32 devices in a mesh: dp: 4 (over z), seq: 8 (over y, x, core).
Axes of the slice: x: 2, y: 2, z: 4, core: 2. Of those that a mesh axis runs over, the one named last changes fastest.
Arguments:
- tokens: bfloat16 [4096, 2048], P(('dp', 'seq')), may hold values from -6 to 6
- cotangent: bfloat16 [4096, 2048], P(('dp', 'seq')), may hold values from -9 to 9
- lengths: int32 [4, 1], P('dp'), may hold values from 0 to 1024, as said below
- query_key_value_weight: float32 [2048, 2560], P(('dp', 'seq')), may hold values from -0.1875 to 0.1875
- out_weight: float32 [2048, 2048], P(None, ('dp', 'seq')), may hold values from -0.5 to 0.5
- gate_up_weight: float32 [2048, 2, 5632], P('dp', None, 'seq'), may hold values from -0.125 to 0.125
- down_weight: float32 [5632, 2048], P('seq', 'dp'), may hold values from -0.078125 to 0.078125
- gains: float32 [2, 2048], P(None, ('dp', 'seq')), may hold values from 0.35 to 3.3
- first_moment_query_key_value: float32 [2048, 2560], P(('dp', 'seq')), may hold values from -0.00010681152 to 0.00010681152
- first_out: float32 [2048, 2048], P(None, ('dp', 'seq')), may hold values from -0.00010681152 to 0.00010681152
- first_gate_up: float32 [2048, 2, 5632], P('dp', None, 'seq'), may hold values from -0.00010681152 to 0.00010681152
- first_down: float32 [5632, 2048], P('seq', 'dp'), may hold values from -0.00010681152 to 0.00010681152
- first_gains: float32 [2, 2048], P(None, ('dp', 'seq')), may hold values from -0.00030517578 to 0.00030517578
- second_moment_query_key_value: float32 [2048, 2560], P(('dp', 'seq')), may hold values from 1.1942525e-09 to 4.7679283e-09
- second_out: float32 [2048, 2048], P(None, ('dp', 'seq')), may hold values from 1.1942525e-09 to 4.7679283e-09
- second_gate_up: float32 [2048, 2, 5632], P('dp', None, 'seq'), may hold values from 1.1942525e-09 to 4.7679283e-09
- second_down: float32 [5632, 2048], P('seq', 'dp'), may hold values from 1.1942525e-09 to 4.7679283e-09
- second_gains: float32 [2, 2048], P(None, ('dp', 'seq')), may hold values from 1.0671077e-08 to 4.3138396e-08
- average_query_key_value: float32 [2048, 2560], P(('dp', 'seq')), may hold values from -0.1875 to 0.1875
- average_out: float32 [2048, 2048], P(None, ('dp', 'seq')), may hold values from -0.5 to 0.5
- average_gate_up: float32 [2048, 2, 5632], P('dp', None, 'seq'), may hold values from -0.125 to 0.125
- average_down: float32 [5632, 2048], P('seq', 'dp'), may hold values from -0.078125 to 0.078125
- average_gains: float32 [2, 2048], P(None, ('dp', 'seq')), may hold values from 0.5 to 1.5
Outputs:
- output: bfloat16 [4096, 2048], P(('dp', 'seq'))
- input_grad: float32 [4096, 2048], P(('dp', 'seq'))
- grad_norm: float32 [], replicated
- grad_qkv: float32 [2048, 2560], P(('dp', 'seq'))
- grad_out: float32 [2048, 2048], P(None, ('dp', 'seq'))
- grad_gate_up: float32 [2048, 2, 5632], P('dp', None, 'seq')
- grad_down: float32 [5632, 2048], P('seq', 'dp')
- grad_gains: float32 [2, 2048], P(None, ('dp', 'seq'))
- new_qkv: float32 [2048, 2560], P(('dp', 'seq'))
- new_out: float32 [2048, 2048], P(None, ('dp', 'seq'))
- new_gate_up: float32 [2048, 2, 5632], P('dp', None, 'seq')
- new_down: float32 [5632, 2048], P('seq', 'dp')
- new_gains: float32 [2, 2048], P(None, ('dp', 'seq'))
- moment_qkv: float32 [2048, 2560], P(('dp', 'seq'))
- moment_out: float32 [2048, 2048], P(None, ('dp', 'seq'))
- moment_gate_up: float32 [2048, 2, 5632], P('dp', None, 'seq')
- moment_down: float32 [5632, 2048], P('seq', 'dp')
- moment_gains: float32 [2, 2048], P(None, ('dp', 'seq'))
- square_qkv: float32 [2048, 2560], P(('dp', 'seq'))
- square_out: float32 [2048, 2048], P(None, ('dp', 'seq'))
- square_gate_up: float32 [2048, 2, 5632], P('dp', None, 'seq')
- square_down: float32 [5632, 2048], P('seq', 'dp')
- square_gains: float32 [2, 2048], P(None, ('dp', 'seq'))
- ema_qkv: float32 [2048, 2560], P(('dp', 'seq'))
- ema_out: float32 [2048, 2048], P(None, ('dp', 'seq'))
- ema_gate_up: float32 [2048, 2, 5632], P('dp', None, 'seq')
- ema_down: float32 [5632, 2048], P('seq', 'dp')
- ema_gains: float32 [2, 2048], P(None, ('dp', 'seq'))
The draws below stay inside these ranges and needn't reach their ends.
Inputs may be any that keep to these rules, and one draw needn't show every extreme that they name: Each row lists one group's document lengths in packing order: multiples of 1024, nonzero ones first and zeros after, summing to 1024; in every draw some group holds one document of 1024 tokens.
All inputs are finite; a program needn't handle non-finite values.
Results may differ from the reference program's by a relative error of at most 0.018.
The reference program's roundings to bfloat16 on the way count: a program that leaves them out, or rounds other values in their place, can miss the bound.
Values may be sent and summed in bfloat16 or wider, within the bound.
No kernel may reach another device: no remote copies, remote signals or barrier semaphores. Data moves between devices by JAX's collectives and lax.ppermute only.
A program may use at most 512 MiB of HBM per device.

```python
import math
import jax
import jax.numpy as jnp
from jax import lax

MODEL_WIDTH = 2048
FF = 5632
QUERY_HEAD_COUNT = 32
KEY_VALUE_HEADS = 4
HEAD_SIZE = 64
SEQ_MIN = 1024
STEP = 10
GTOK = 1024
TOKENS = 4096
SLOTS = 1
LAYER_PARAMETERS = 44044288


def draw_lengths(key, part):
    key = jax.random.fold_in(key, 11)
    groups = TOKENS // GTOK
    cut_key, pick_key = jax.random.split(key)
    cut_bits = jax.random.randint(cut_key, (groups, SLOTS - 1), 0, 2).astype(jnp.int32)
    single = jax.random.randint(pick_key, (), 0, groups)
    group_ids = jnp.arange(groups, dtype=jnp.int32)[:, None]
    cut_bits = jnp.where(group_ids == single, 0, cut_bits)
    unit_segment = jnp.concatenate([jnp.zeros((groups, 1), jnp.int32), jnp.cumsum(cut_bits, axis=1).astype(jnp.int32)], axis=1)
    slot_ids = jnp.arange(SLOTS, dtype=jnp.int32)
    unit_counts = jnp.sum((unit_segment[:, :, None] == slot_ids[None, None, :]).astype(jnp.int32), axis=1)
    return (unit_counts * SEQ_MIN).astype(jnp.int32)


def draw_gains(key, part):
    key = jax.random.fold_in(key, 21)
    ramp_pos = jnp.arange(MODEL_WIDTH, dtype=jnp.float32) / (MODEL_WIDTH - 1)
    ramp_scale = 0.6 * 3.0 ** ramp_pos
    jitter = jnp.exp(jax.random.uniform(key, (2, MODEL_WIDTH), jnp.float32, -0.22, 0.22))
    return ramp_scale[None, :] * jitter


def draw_cotangent(key, part):
    key = jax.random.fold_in(key, 31)
    ramp_pos = jnp.arange(MODEL_WIDTH, dtype=jnp.float32) / (MODEL_WIDTH - 1)
    ramp_scale = 0.6 * 3.0 ** ramp_pos
    entries = jnp.clip(jax.random.normal(key, (TOKENS, MODEL_WIDTH), jnp.float32), -5.0, 5.0)
    return (entries * ramp_scale[None, :]).astype(jnp.bfloat16)


def steps_of(rng, dims, shards, least, top_value):
    loudness = 1.0
    for axis_at, shards_of in shards:
        heights = jax.random.uniform(jax.random.fold_in(jax.random.fold_in(rng, 6), axis_at), (shards_of,), jnp.float32, least / len(shards), top_value / len(shards))
        loudness = loudness * jnp.repeat(jnp.exp(heights), dims[axis_at] // shards_of).reshape((-1,) + (1,) * (len(dims) - 1 - axis_at))
    return loudness


def centred(own_key, dims, scale, bound, cuts=(), kind=jnp.bfloat16):
    loudness = steps_of(own_key, dims, cuts, -0.22, 0.18) if cuts else 1.0
    values = jax.random.normal(own_key, dims, jnp.float32) * scale * loudness
    return jnp.minimum(jnp.maximum(values, -bound), bound).astype(kind)


def setup_inputs(seed: int = 0) -> dict:
    streams_of = jax.random.split(jax.random.key(seed), 24)
    return {
        "tokens": centred(streams_of[0], (TOKENS, MODEL_WIDTH), 1.0, 6.0, ((0, 32),)),
        "cotangent": draw_cotangent(jax.random.fold_in(streams_of[23], 71), 0),
        "lengths": draw_lengths(jax.random.fold_in(streams_of[23], 71), 0),
        "query_key_value_weight": centred(streams_of[3], (MODEL_WIDTH, (QUERY_HEAD_COUNT + 2 * KEY_VALUE_HEADS) * HEAD_SIZE), (MODEL_WIDTH // 2) ** -0.5, 0.1875, ((0, 32),), jnp.float32),
        "out_weight": centred(streams_of[4], (QUERY_HEAD_COUNT * HEAD_SIZE, MODEL_WIDTH), (QUERY_HEAD_COUNT * HEAD_SIZE // 16) ** -0.5, 0.5, ((1, 32),), jnp.float32),
        "gate_up_weight": centred(streams_of[5], (MODEL_WIDTH, 2, FF), MODEL_WIDTH ** -0.5, 0.125, ((0, 4), (2, 8)), jnp.float32),
        "down_weight": centred(streams_of[6], (FF, MODEL_WIDTH), FF ** -0.5, 0.078125, ((0, 8), (1, 4)), jnp.float32),
        "gains": draw_gains(jax.random.fold_in(streams_of[23], 71), 0),
        "first_moment_query_key_value": centred(streams_of[8], (MODEL_WIDTH, (QUERY_HEAD_COUNT + 2 * KEY_VALUE_HEADS) * HEAD_SIZE), (0.111 / LAYER_PARAMETERS ** 0.5), 0.00010681152, ((0, 32),), jnp.float32),
        "first_out": centred(streams_of[9], (QUERY_HEAD_COUNT * HEAD_SIZE, MODEL_WIDTH), (0.111 / LAYER_PARAMETERS ** 0.5), 0.00010681152, ((1, 32),), jnp.float32),
        "first_gate_up": centred(streams_of[10], (MODEL_WIDTH, 2, FF), (0.111 / LAYER_PARAMETERS ** 0.5), 0.00010681152, ((0, 4), (2, 8)), jnp.float32),
        "first_down": centred(streams_of[11], (FF, MODEL_WIDTH), (0.111 / LAYER_PARAMETERS ** 0.5), 0.00010681152, ((0, 8), (1, 4)), jnp.float32),
        "first_gains": centred(streams_of[12], (2, MODEL_WIDTH), (0.333 / LAYER_PARAMETERS ** 0.5), 0.00030517578, ((1, 32),), jnp.float32),
        "second_moment_query_key_value": jnp.clip(jnp.exp(math.log(4.767928274418409e-09) - 1.3843914 * jax.random.uniform(streams_of[13], (MODEL_WIDTH, (QUERY_HEAD_COUNT + 2 * KEY_VALUE_HEADS) * HEAD_SIZE), jnp.float32) ** steps_of(streams_of[13], (MODEL_WIDTH, (QUERY_HEAD_COUNT + 2 * KEY_VALUE_HEADS) * HEAD_SIZE), ((0, 32),), -0.2, 0.2)), 1.1942524746899608e-09, 4.767928274418409e-09),
        "second_out": jnp.clip(jnp.exp(math.log(4.767928274418409e-09) - 1.3843914 * jax.random.uniform(streams_of[14], (QUERY_HEAD_COUNT * HEAD_SIZE, MODEL_WIDTH), jnp.float32) ** steps_of(streams_of[14], (QUERY_HEAD_COUNT * HEAD_SIZE, MODEL_WIDTH), ((1, 32),), -0.2, 0.2)), 1.1942524746899608e-09, 4.767928274418409e-09),
        "second_gate_up": jnp.clip(jnp.exp(math.log(4.767928274418409e-09) - 1.3843914 * jax.random.uniform(streams_of[15], (MODEL_WIDTH, 2, FF), jnp.float32) ** steps_of(streams_of[15], (MODEL_WIDTH, 2, FF), ((0, 4), (2, 8)), -0.2, 0.2)), 1.1942524746899608e-09, 4.767928274418409e-09),
        "second_down": jnp.clip(jnp.exp(math.log(4.767928274418409e-09) - 1.3843914 * jax.random.uniform(streams_of[16], (FF, MODEL_WIDTH), jnp.float32) ** steps_of(streams_of[16], (FF, MODEL_WIDTH), ((0, 8), (1, 4)), -0.2, 0.2)), 1.1942524746899608e-09, 4.767928274418409e-09),
        "second_gains": jnp.clip(jnp.exp(math.log(4.313839596647995e-08) - 1.3968764 * jax.random.uniform(streams_of[17], (2, MODEL_WIDTH), jnp.float32) ** steps_of(streams_of[17], (2, MODEL_WIDTH), ((1, 32),), -0.2, 0.2)), 1.0671077355084435e-08, 4.313839596647995e-08),
        "average_query_key_value": centred(streams_of[18], (MODEL_WIDTH, (QUERY_HEAD_COUNT + 2 * KEY_VALUE_HEADS) * HEAD_SIZE), (MODEL_WIDTH // 2) ** -0.5, 0.1875, ((0, 32),), jnp.float32),
        "average_out": centred(streams_of[19], (QUERY_HEAD_COUNT * HEAD_SIZE, MODEL_WIDTH), (QUERY_HEAD_COUNT * HEAD_SIZE // 16) ** -0.5, 0.5, ((1, 32),), jnp.float32),
        "average_gate_up": centred(streams_of[20], (MODEL_WIDTH, 2, FF), MODEL_WIDTH ** -0.5, 0.125, ((0, 4), (2, 8)), jnp.float32),
        "average_down": centred(streams_of[21], (FF, MODEL_WIDTH), FF ** -0.5, 0.078125, ((0, 8), (1, 4)), jnp.float32),
        "average_gains": jnp.clip(1.0 + 0.1 * jax.random.normal(streams_of[22], (2, MODEL_WIDTH), jnp.float32), 0.5, 1.5),
    }


rms_eps = 1e-05
rope_base = 10000.0
clip_limit = 1.0
beta_one = 0.9
beta_two = 0.95
adam_eps = 1e-08
weight_decay = 0.1
ema_decay = 0.8
masked_score = -1e+30

@jax.custom_vjp
def low(v):
    return lax.optimization_barrier(v.astype(jnp.bfloat16)).astype(jnp.float32)

@jax.custom_vjp
def low_back(v):
    return v

def low_keep(v):
    return (low(v), None)

def low_pass(kept, grad):
    return (grad,)

def back_keep(v):
    return (v, None)

def back_low(kept, grad):
    return (low(grad),)
low.defvjp(low_keep, low_pass)
low_back.defvjp(back_keep, back_low)

def matmul(left, right):
    return jnp.dot(left, right, precision=lax.Precision.HIGHEST, preferred_element_type=jnp.float32)

def rms_scale(inputs, gain_row):
    inverse = lax.rsqrt(lax.optimization_barrier(jnp.mean(inputs * inputs, axis=-1, keepdims=True)) + rms_eps)
    return inputs * inverse * gain_row

def rotate(field, cosine, sine):
    half_width = field.shape[-1] // 2
    turned = jnp.concatenate([-field[..., half_width:], field[..., :half_width]], axis=-1)
    return field * cosine + turned * sine

def angles(positions, head_width):
    frequency = rope_base ** (-2.0 * jnp.arange(head_width // 2, dtype=jnp.float32) / head_width)
    phases = positions.astype(jnp.float32)[:, None] * frequency[None, :]
    phases = jnp.concatenate([phases, phases], axis=-1)
    return (jnp.cos(phases)[:, None, :], jnp.sin(phases)[:, None, :])

def swiglu(gate_up):
    half_width = gate_up.shape[-1] // 2
    gate_half = gate_up[:, :half_width]
    return gate_half * jax.nn.sigmoid(gate_half) * gate_up[:, half_width:]

def layout(lengths_row, group_length):
    seq_ends = jnp.cumsum(lengths_row).astype(jnp.int32)
    places = jnp.arange(group_length, dtype=jnp.int32)
    segment = lax.optimization_barrier(jnp.sum((places[:, None] >= seq_ends[None, :]).astype(jnp.int32), axis=1)).astype(jnp.int32)
    seq_starts = (seq_ends - lengths_row).astype(jnp.int32)
    slot_ids = jnp.arange(seq_ends.shape[0], dtype=jnp.int32)
    seq_begin = lax.optimization_barrier(jnp.sum(jnp.where(segment[:, None] == slot_ids[None, :], seq_starts[None, :], 0), axis=1)).astype(jnp.int32)
    return (segment, (places - seq_begin).astype(jnp.int32))

def attend(queries, key_heads, value_heads, segment, score_scale):
    group_length = queries.shape[0]
    block_size = min(512, group_length)
    places = jnp.arange(group_length, dtype=jnp.int32)

    def one_block(block_index):
        row_start = block_index * block_size
        row_block = lax.dynamic_slice_in_dim(queries, row_start, block_size, 0)
        row_segment = lax.dynamic_slice_in_dim(segment, row_start, block_size, 0)
        row_places = row_start + jnp.arange(block_size, dtype=jnp.int32)
        scores = low_back(jnp.einsum('qhd,khd->hqk', row_block, key_heads, precision=lax.Precision.HIGHEST) * score_scale)
        allowed = (row_segment[:, None] == segment[None, :]) & (places[None, :] <= row_places[:, None])
        scores = jnp.where(allowed[None], scores, masked_score)
        row_peak = lax.optimization_barrier(jnp.max(scores, axis=-1, keepdims=True))
        logsum = row_peak + jnp.log(lax.optimization_barrier(jnp.sum(jnp.exp(scores - row_peak), axis=-1, keepdims=True)))
        weights = low(jnp.exp(scores - logsum))
        return jnp.einsum('hqk,khd->qhd', weights, value_heads, precision=lax.Precision.HIGHEST)
    out_blocks = lax.map(jax.checkpoint(one_block), jnp.arange(group_length // block_size, dtype=jnp.int32))
    return out_blocks.reshape(group_length, queries.shape[1], queries.shape[2])

def group_layer(group_rows, segment, positions, rounded):
    qkv_w, out_w, gate_up_w, down_w, gain_pair = rounded
    group_length = group_rows.shape[0]
    normed = low(rms_scale(group_rows, gain_pair[0]))
    mixed_projection = low_back(matmul(normed, qkv_w))
    query_raw = mixed_projection[:, :QUERY_HEAD_COUNT * HEAD_SIZE].reshape(group_length, QUERY_HEAD_COUNT, HEAD_SIZE)
    key_unrotated = mixed_projection[:, QUERY_HEAD_COUNT * HEAD_SIZE:(QUERY_HEAD_COUNT + KEY_VALUE_HEADS) * HEAD_SIZE].reshape(group_length, KEY_VALUE_HEADS, HEAD_SIZE)
    value_unrotated = mixed_projection[:, (QUERY_HEAD_COUNT + KEY_VALUE_HEADS) * HEAD_SIZE:].reshape(group_length, KEY_VALUE_HEADS, HEAD_SIZE)
    cosine, sine = angles(positions, HEAD_SIZE)
    queries = low(low_back(rotate(query_raw, cosine, sine)))
    key_rot = low(rotate(key_unrotated, cosine, sine))
    values = low(value_unrotated)
    repeat_factor_count = QUERY_HEAD_COUNT // KEY_VALUE_HEADS
    attended = attend(queries, jnp.repeat(key_rot, repeat_factor_count, axis=1), jnp.repeat(values, repeat_factor_count, axis=1), segment, HEAD_SIZE ** (-0.5))
    attended = low(low_back(attended.reshape(group_length, QUERY_HEAD_COUNT * HEAD_SIZE)))
    middle = group_rows + low_back(matmul(attended, out_w))
    normed_two = low(rms_scale(middle, gain_pair[1]))
    gate_up = low_back(matmul(normed_two, gate_up_w.reshape(gate_up_w.shape[0], -1)))
    hidden = low(swiglu(gate_up))
    return middle + low_back(matmul(hidden, down_w))

def block_layer(inputs, masters, segment, positions):
    rounded = tuple((low(master) for master in masters))
    group_fn = jax.checkpoint(group_layer)

    def per_group(pieces):
        return group_fn(pieces[0], pieces[1], pieces[2], rounded)
    groups = segment.shape[0]
    out_groups = lax.map(per_group, (inputs.reshape(groups, -1, inputs.shape[1]), segment, positions))
    return out_groups.reshape(inputs.shape)

def rates():
    return (0.5 * (2.0 / MODEL_WIDTH) ** 0.5, 0.5 * (16.0 / (QUERY_HEAD_COUNT * HEAD_SIZE)) ** 0.5, 0.5 * (1.0 / MODEL_WIDTH) ** 0.5, 0.5 * (1.0 / FF) ** 0.5, 0.3)

def adam_update(weight, gradient, moment_one, moment_two, average, rate):
    first_new = beta_one * moment_one + (1.0 - beta_one) * gradient
    second_new = beta_two * moment_two + (1.0 - beta_two) * gradient * gradient
    corrected = first_new / (1.0 - beta_one ** STEP) / (jnp.sqrt(second_new / (1.0 - beta_two ** STEP)) + adam_eps)
    weight_new = weight - rate * (corrected + weight_decay * weight)
    average_new = ema_decay * average + (1.0 - ema_decay) * weight_new
    return (weight_new, first_new, second_new, average_new)

def reference(tokens, cotangent, lengths, query_key_value_weight, out_weight, gate_up_weight, down_weight, gains, first_moment_query_key_value, first_out, first_gate_up, first_down, first_gains, second_moment_query_key_value, second_out, second_gate_up, second_down, second_gains, average_query_key_value, average_out, average_gate_up, average_down, average_gains):
    segment, positions = jax.vmap(lambda lengths_row: layout(lengths_row, GTOK))(lengths)

    def forward(inputs, qkv_w, out_w, gate_up_w, down_w, gain_w):
        return block_layer(inputs, (qkv_w, out_w, gate_up_w, down_w, gain_w), segment, positions)
    output, backward = jax.vjp(forward, tokens.astype(jnp.float32), query_key_value_weight, out_weight, gate_up_weight, down_weight, gains)
    gradients = backward(cotangent.astype(jnp.float32))
    input_grad = gradients[0]
    weight_grads = gradients[1:]
    total_square = sum((jnp.sum(gradient * gradient) for gradient in weight_grads))
    grad_norm = jnp.sqrt(total_square)
    factor = jnp.minimum(1.0, clip_limit / grad_norm)
    clipped = tuple((factor * gradient for gradient in weight_grads))
    masters = (query_key_value_weight, out_weight, gate_up_weight, down_weight, gains)
    firsts = (first_moment_query_key_value, first_out, first_gate_up, first_down, first_gains)
    seconds = (second_moment_query_key_value, second_out, second_gate_up, second_down, second_gains)
    averages = (average_query_key_value, average_out, average_gate_up, average_down, average_gains)
    results = [adam_update(masters[slot], clipped[slot], firsts[slot], seconds[slot], averages[slot], rates()[slot]) for slot in range(5)]
    return (output.astype(jnp.bfloat16), input_grad, grad_norm, clipped[0], clipped[1], clipped[2], clipped[3], clipped[4], results[0][0], results[1][0], results[2][0], results[3][0], results[4][0], results[0][1], results[1][1], results[2][1], results[3][1], results[4][1], results[0][2], results[1][2], results[2][2], results[3][2], results[4][2], results[0][3], results[1][3], results[2][3], results[3][3], results[4][3])
```

```python
import functools

import jax
import jax.numpy as jnp
from jax import lax
from jax.experimental import pallas as pl
from jax.experimental.pallas import tpu as pltpu
from jax.sharding import PartitionSpec as P

MODEL_WIDTH = 2048
FF = 5632
QUERY_HEAD_COUNT = 32
KEY_VALUE_HEADS = 4
HEAD_SIZE = 64
STEP = 10

rms_eps = 1e-05
rope_base = 10000.0
clip_limit = 1.0
beta_one = 0.9
beta_two = 0.95
adam_eps = 1e-08
weight_decay = 0.1
ema_decay = 0.8
masked_score = -1e30

HALF = HEAD_SIZE // 2
SCALE = HEAD_SIZE ** (-0.5)
F32 = jnp.float32
BF16 = jnp.bfloat16


def dot(left, right, left_dim, right_dim):
    return lax.dot_general(
        left, right, (((left_dim,), (right_dim,)), ((), ())), preferred_element_type=F32
    )


def swap(value, mask):
    count = lax.axis_size("seq")
    return lax.ppermute(value, "seq", [(at, at ^ mask) for at in range(count)])


def seq_gather(rows):
    count = lax.axis_size("seq")
    if count != 8:
        return jnp.concatenate([rows] + [swap(rows, mask) for mask in range(1, count)], axis=0)
    half = rows.shape[0] // 2
    by_x, by_y, by_core = swap(rows, 2), swap(rows, 4), swap(rows, 1)
    upper, lower = swap(by_x[:half], 4), swap(by_y[half:], 2)
    return jnp.concatenate(
        [
            rows,
            by_core,
            by_x,
            swap(by_x, 1),
            by_y,
            swap(by_y, 1),
            upper,
            lower,
            swap(upper, 1),
            swap(lower, 1),
        ],
        axis=0,
    )


def seq_scatter(partial):
    count = lax.axis_size("seq")
    size = partial.shape[0] // count

    def slot(mask):
        return partial[mask * size : (mask + 1) * size]

    if count != 8:
        total = slot(0).astype(F32)
        for mask in range(1, count):
            total = total + swap(slot(mask), mask).astype(F32)
        return total
    half = size // 2
    other = swap(jnp.concatenate([slot(7), slot(3), slot(5), slot(1)], axis=0), 1).astype(F32)
    diagonal = slot(6).astype(F32) + other[:size]
    by_x = slot(2).astype(F32) + other[size : 2 * size]
    by_y = slot(4).astype(F32) + other[2 * size : 3 * size]
    mine = slot(0).astype(F32) + other[3 * size :]
    first_x = swap(jnp.concatenate([diagonal[:half], by_x[:half]], axis=0).astype(BF16), 2)
    first_y = swap(jnp.concatenate([diagonal[half:], by_y[half:]], axis=0).astype(BF16), 4)
    second_x = swap((by_x[half:] + first_y[:half].astype(F32)).astype(BF16), 2)
    second_y = swap((by_y[:half] + first_x[:half].astype(F32)).astype(BF16), 4)
    upper = first_x[half:].astype(F32) + second_y.astype(F32)
    lower = second_x.astype(F32) + first_y[half:].astype(F32)
    return mine + jnp.concatenate([upper, lower], axis=0)


def shift(value, step):
    count = lax.axis_size("dp")
    return lax.ppermute(value, "dp", [(at, (at + step) % count) for at in range(count)])


def dp_gather(own):
    count = lax.axis_size("dp")
    if count != 4:
        return [own] + [shift(own, -k) for k in range(1, count)]
    after, before = shift(own, -1), shift(own, 1)
    from_after = lax.ppermute(after, "dp", [(1, 0), (2, 1)])
    from_before = lax.ppermute(before, "dp", [(1, 2), (2, 3)])
    across = jnp.where(lax.axis_index("dp") < 2, from_after, from_before)
    return [own, after, across, before]


def dp_scatter(blocks):
    count = lax.axis_size("dp")
    kind = blocks[0].dtype
    if count != 4:
        total = blocks[0].astype(F32)
        for k in range(1, count):
            total = total + shift(blocks[k], k).astype(F32)
        return total
    up = lax.ppermute(blocks[2], "dp", [(0, 1), (1, 2)])
    down = lax.ppermute(blocks[2], "dp", [(3, 2), (2, 1)])
    after = shift((blocks[1].astype(F32) + up.astype(F32)).astype(kind), 1)
    before = shift((blocks[3].astype(F32) + down.astype(F32)).astype(kind), -1)
    return blocks[0].astype(F32) + after.astype(F32) + before.astype(F32)


def turn_columns(value, step):
    count = lax.axis_size("dp")
    block = value.shape[1] // count
    return lax.select_n(step, *[jnp.roll(value, -k * block, axis=1) for k in range(count)])


def block_rows(length):
    return min(256, length)


def slot_span(seq_ref, chunk, size):
    return pl.ds(pl.multiple_of(lax.bitwise_xor(seq_ref[0], chunk) * size, size), size)


def allowed_pairs(start_ref, documents, row_from, width, rows):
    key_at = lax.broadcasted_iota(jnp.int32, (width, rows), 0)
    query_at = row_from + lax.broadcasted_iota(jnp.int32, (width, rows), 1)
    allowed = key_at <= query_at
    if documents > 1:
        allowed = allowed & (key_at >= start_ref[:, row_from : row_from + rows])
    return allowed


def forward_kernel(
    heads,
    size,
    documents,
    seq_ref,
    start_ref,
    mixed_ref,
    cos_ref,
    sin_ref,
    out_ref,
    query_ref,
    key_ref,
    key_t_ref,
    value_ref,
    value_t_ref,
    lse_ref,
    gathered,
):
    length = mixed_ref.shape[1]
    width = heads * HEAD_SIZE
    for chunk in range(length // size):
        source = slot_span(seq_ref, chunk, size)
        place = slice(chunk * size, (chunk + 1) * size)
        cosine, sine = cos_ref[:, place], sin_ref[:, place]
        for head in range(heads + 1):
            base = head * HEAD_SIZE
            one = mixed_ref[base : base + HALF, source]
            two = mixed_ref[base + HALF : base + HEAD_SIZE, source]
            turned = jnp.concatenate(
                [one * cosine - two * sine, two * cosine + one * sine], axis=0
            ).astype(BF16)
            if head < heads:
                query_ref[base : base + HEAD_SIZE, place] = turned
            else:
                key_t_ref[:, place] = turned
        value_t_ref[:, place] = mixed_ref[width + HEAD_SIZE : width + 2 * HEAD_SIZE, source].astype(
            BF16
        )
    key_ref[...] = key_t_ref[...].astype(F32).T.astype(BF16)
    value_ref[...] = value_t_ref[...].astype(F32).T.astype(BF16)
    rows = block_rows(length)
    for block in range(length // rows):
        place = slice(block * rows, (block + 1) * rows)
        reach = (block + 1) * rows
        allowed = allowed_pairs(start_ref, documents, block * rows, reach, rows)
        for head in range(heads):
            span = slice(head * HEAD_SIZE, (head + 1) * HEAD_SIZE)
            query = query_ref[span, place] * jnp.asarray(SCALE, BF16)
            scores = jnp.where(allowed, dot(key_ref[:reach], query, 1, 0), masked_score)
            peak = jnp.max(scores, axis=0, keepdims=True)
            raised = jnp.exp(scores - peak)
            total = jnp.sum(raised, axis=0, keepdims=True)
            lse_ref[head : head + 1, place] = peak + jnp.log(total)
            weights = (raised * (1.0 / total)).astype(BF16)
            gathered[span, :] = dot(value_t_ref[:, :reach], weights, 1, 0)
        out = gathered[...].T.astype(BF16)
        for piece in range(rows // size):
            target = slot_span(seq_ref, block * (rows // size) + piece, size)
            out_ref[target, :] = out[piece * size : (piece + 1) * size]


def backward_kernel(
    heads,
    share,
    size,
    documents,
    seq_ref,
    start_ref,
    query_ref,
    key_ref,
    key_t_ref,
    value_ref,
    lse_ref,
    grad_ref,
    cos_ref,
    sin_ref,
    grad_query_ref,
    grad_pair_ref,
    grad_key,
    grad_value,
):
    length = query_ref.shape[1]
    rows = block_rows(length)
    pieces = rows // size
    grad_key[...] = jnp.zeros_like(grad_key)
    grad_value[...] = jnp.zeros_like(grad_value)
    for block in range(length // rows):
        place = slice(block * rows, (block + 1) * rows)
        reach = (block + 1) * rows
        allowed = allowed_pairs(start_ref, documents, block * rows, reach, rows)
        cosine, sine = cos_ref[:, place], sin_ref[:, place]
        spans = [slot_span(seq_ref, block * pieces + piece, size) for piece in range(pieces)]
        for head in range(heads):
            base = head * HEAD_SIZE
            span = slice(base, base + HEAD_SIZE)
            query = query_ref[span, place] * jnp.asarray(SCALE, BF16)
            grad = jnp.concatenate([grad_ref[span, where] for where in spans], axis=1)
            scores = jnp.where(allowed, dot(key_ref[:reach], query, 1, 0), masked_score)
            weights = jnp.exp(scores - lse_ref[head : head + 1, place])
            slope = dot(value_ref[:reach], grad, 1, 0)
            delta = jnp.sum(weights * slope, axis=0, keepdims=True)
            inner = (weights * (slope - delta)).astype(BF16)
            pulled = (dot(key_t_ref[:, :reach], inner, 1, 0) * SCALE).astype(BF16).astype(F32)
            one, two = pulled[:HALF], pulled[HALF:]
            turned = jnp.concatenate(
                [one * cosine + two * sine, two * cosine - one * sine], axis=0
            ).astype(BF16)
            for piece, where in enumerate(spans):
                grad_query_ref[span, where] = turned[:, piece * size : (piece + 1) * size]
            grad_key[:reach] += dot(inner, query, 1, 1)
            grad_value[:reach] += dot(weights.astype(BF16), grad, 1, 1)
    key_t = grad_key[...].T
    value_t = grad_value[...].T
    one, two = key_t[:HALF], key_t[HALF:]
    cosine, sine = cos_ref[...], sin_ref[...]
    turned = jnp.concatenate([one * cosine + two * sine, two * cosine - one * sine], axis=0)
    both = jnp.concatenate([turned, value_t], axis=0)
    kept = 2 * HEAD_SIZE // share
    first_sharer = seq_ref[0] - lax.rem(seq_ref[0], share)
    for sharer in range(share):
        span = slice(sharer * kept, (sharer + 1) * kept)
        for chunk in range(length // size):
            slot = lax.bitwise_xor(first_sharer + sharer, chunk)
            target = pl.ds(pl.multiple_of(slot * size, size), size)
            grad_pair_ref[span, target] = both[span, chunk * size : (chunk + 1) * size]


def attention_cost(heads, length, dots):
    return pl.CostEstimate(
        flops=dots * heads * length * length * 256,
        bytes_accessed=8 * length * heads * HEAD_SIZE,
        transcendentals=heads * length * length,
    )


def vmem_specs(count):
    return [pl.BlockSpec(memory_space=pltpu.VMEM)] * count


def attention_forward(seq_at, starts, mixed, cosine, sine, heads, size, documents):
    length = mixed.shape[1]
    width = heads * HEAD_SIZE
    shape = jax.ShapeDtypeStruct
    return pl.pallas_call(
        functools.partial(forward_kernel, heads, size, documents),
        out_shape=[
            shape((length, width), BF16),
            shape((width, length), BF16),
            shape((length, HEAD_SIZE), BF16),
            shape((HEAD_SIZE, length), BF16),
            shape((length, HEAD_SIZE), BF16),
            shape((HEAD_SIZE, length), BF16),
            shape((8, length), F32),
        ],
        in_specs=[pl.BlockSpec(memory_space=pltpu.SMEM)] + vmem_specs(4),
        out_specs=vmem_specs(7),
        scratch_shapes=[pltpu.VMEM((width, block_rows(length)), F32)],
        compiler_params=pltpu.CompilerParams(vmem_limit_bytes=40 << 20),
        cost_estimate=attention_cost(heads, length, 2),
        name="attention_forward",
    )(seq_at, starts, mixed, cosine, sine)


def attention_backward(
    seq_at, starts, query, key, key_t, value, lse, grad, cosine, sine, heads, share, size, documents
):
    width, length = query.shape
    shape = jax.ShapeDtypeStruct
    return pl.pallas_call(
        functools.partial(backward_kernel, heads, share, size, documents),
        out_shape=[shape((width, length), BF16), shape((2 * HEAD_SIZE, length), F32)],
        in_specs=[pl.BlockSpec(memory_space=pltpu.SMEM)] + vmem_specs(9),
        out_specs=vmem_specs(2),
        scratch_shapes=[pltpu.VMEM((length, HEAD_SIZE), F32)] * 2,
        compiler_params=pltpu.CompilerParams(vmem_limit_bytes=40 << 20),
        cost_estimate=attention_cost(heads, length, 5),
        name="attention_backward",
    )(seq_at, starts, query, key, key_t, value, lse, grad, cosine, sine)


def rates():
    return (
        0.5 * (2.0 / MODEL_WIDTH) ** 0.5,
        0.5 * (16.0 / (QUERY_HEAD_COUNT * HEAD_SIZE)) ** 0.5,
        0.5 * (1.0 / MODEL_WIDTH) ** 0.5,
        0.5 * (1.0 / FF) ** 0.5,
        0.3,
    )


def adam_update(weight, gradient, moment_one, moment_two, average, rate):
    first_new = beta_one * moment_one + (1.0 - beta_one) * gradient
    second_new = beta_two * moment_two + (1.0 - beta_two) * gradient * gradient
    corrected = (
        first_new
        / (1.0 - beta_one**STEP)
        / (jnp.sqrt(second_new / (1.0 - beta_two**STEP)) + adam_eps)
    )
    weight_new = weight - rate * (corrected + weight_decay * weight)
    average_new = ema_decay * average + (1.0 - ema_decay) * weight_new
    return (weight_new, first_new, second_new, average_new)


def on_device(
    tokens,
    cotangent,
    lengths,
    query_key_value_weight,
    out_weight,
    gate_up_weight,
    down_weight,
    gains,
    first_moment_query_key_value,
    first_out,
    first_gate_up,
    first_down,
    first_gains,
    second_moment_query_key_value,
    second_out,
    second_gate_up,
    second_down,
    second_gains,
    average_query_key_value,
    average_out,
    average_gate_up,
    average_down,
    average_gains,
):
    planes, lanes = lax.axis_size("dp"), lax.axis_size("seq")
    plane, lane = lax.axis_index("dp"), lax.axis_index("seq")
    size, width = tokens.shape
    length = size * lanes
    documents = lengths.shape[1]
    heads = QUERY_HEAD_COUNT // lanes
    columns = heads * HEAD_SIZE
    share = lanes // KEY_VALUE_HEADS
    kept = 2 * HEAD_SIZE // share
    every = columns + 2 * HEAD_SIZE
    owned = query_key_value_weight.shape[0]
    block = owned * lanes
    query_width = QUERY_HEAD_COUNT * HEAD_SIZE
    pair_width = KEY_VALUE_HEADS * HEAD_SIZE
    units = gate_up_weight.shape[2]
    seq_at = lane.astype(jnp.int32).reshape(1)

    qkv_b = query_key_value_weight.astype(BF16)
    query_part = qkv_b[:, :query_width].reshape(owned, lanes, columns)

    def per_device(part):
        part = part.reshape(owned, KEY_VALUE_HEADS, HEAD_SIZE)
        return jnp.repeat(part, share, axis=1)

    key_part = per_device(qkv_b[:, query_width : query_width + pair_width])
    value_part = per_device(qkv_b[:, query_width + pair_width :])
    message = jnp.concatenate([query_part, key_part, value_part], axis=2).transpose(1, 0, 2)
    gain_row = jnp.pad(gains.astype(BF16).reshape(1, 2 * owned), ((0, 7), (0, every - 2 * owned)))
    message = jnp.concatenate(
        [message, jnp.broadcast_to(gain_row[None], (lanes, 8, every))], axis=1
    )
    message = lax.all_to_all(message, "seq", split_axis=0, concat_axis=0, tiled=True)
    own_qkv = message[:, :owned].reshape(block, every)
    own_qkv = jnp.concatenate([own_qkv, message[:, owned]], axis=0)
    qkv_pieces = dp_gather(own_qkv)
    qkv_full = jnp.concatenate([piece[:block] for piece in qkv_pieces], axis=0)
    gain_pair = jnp.concatenate(
        [
            piece[block:, : 2 * owned].reshape(lanes, 2, owned).transpose(1, 0, 2).reshape(2, block)
            for piece in qkv_pieces
        ],
        axis=1,
    ).astype(F32)

    in_turned = turn_columns(tokens, plane)
    grad_turned = turn_columns(cotangent, plane)
    in_all = seq_gather(in_turned)
    grad_all = seq_gather(grad_turned)

    out_b = out_weight.T.astype(BF16).reshape(owned, lanes, columns).transpose(1, 0, 2)
    out_b = lax.all_to_all(out_b, "seq", split_axis=0, concat_axis=0, tiled=True)
    out_full = jnp.concatenate(dp_gather(out_b.reshape(block, columns)), axis=0)

    gate_up_b = gate_up_weight.transpose(1, 2, 0).reshape(2 * units, block).astype(BF16)
    gate_up_full = jnp.concatenate(dp_gather(gate_up_b), axis=1)
    down_full = jnp.concatenate(dp_gather(down_weight.astype(BF16)), axis=1)

    ends = jnp.cumsum(lengths[0])
    places = jnp.arange(length, dtype=jnp.int32)
    begins = (ends - lengths[0])[None, :]
    within = (places[:, None] >= begins) & (places[:, None] < ends[None, :])
    starts = jnp.sum(jnp.where(within, begins, 0), axis=1).astype(jnp.int32)
    frequency = rope_base ** (-2.0 * jnp.arange(HALF, dtype=F32) / HEAD_SIZE)
    phases = frequency[:, None] * (places - starts).astype(F32)[None, :]
    cosine, sine = jnp.cos(phases), jnp.sin(phases)
    starts = starts[None, :]

    in_rows = in_all.astype(F32)
    scale_one = lax.rsqrt(jnp.mean(in_rows * in_rows, axis=-1, keepdims=True) + rms_eps)
    normed = (in_rows * scale_one * gain_pair[0]).astype(BF16)
    mixed = dot(qkv_full, normed, 0, 1)
    attended, query, key, key_t, value, _, lse = attention_forward(
        seq_at, starts, mixed, cosine, sine, heads, size, documents
    )
    middle = in_turned.astype(F32) + seq_scatter(dot(attended, out_full, 1, 1).astype(BF16))

    scale_two = lax.rsqrt(jnp.mean(middle * middle, axis=-1, keepdims=True) + rms_eps)
    unit_two = middle * scale_two
    normed_two = seq_gather((unit_two * gain_pair[1]).astype(BF16))
    gate_up = dot(gate_up_full, normed_two, 1, 1)
    gate, up = gate_up[:units], gate_up[units:]
    sigmoid = jax.nn.sigmoid(gate)
    hidden = (gate * sigmoid * up).astype(BF16)
    output = middle + seq_scatter(dot(hidden, down_full, 0, 0).astype(BF16))
    output = turn_columns(output.astype(BF16), (planes - plane) % planes)

    grad_hidden = dot(down_full, grad_all, 1, 1)
    grad_gate = grad_hidden * up * sigmoid * (1.0 + gate * (1.0 - sigmoid))
    grad_up = grad_hidden * gate * sigmoid
    grad_gate_up = jnp.concatenate([grad_gate.astype(BF16), grad_up.astype(BF16)], axis=0)

    def feature_block(array, k):
        return array[:, k * block : (k + 1) * block]

    reduced_down = dp_scatter(
        [dot(hidden, feature_block(grad_all, k), 1, 0).astype(BF16) for k in range(planes)]
    )
    reduced_gate_up = dp_scatter(
        [dot(grad_gate_up, feature_block(normed_two, k), 1, 0).astype(BF16) for k in range(planes)]
    )
    grad_normed_two = seq_scatter(dot(grad_gate_up, gate_up_full, 0, 0).astype(BF16))
    grad_unit = grad_normed_two * gain_pair[1]
    gain_two_sum = jnp.sum(grad_normed_two * unit_two, axis=0)
    grad_middle = grad_turned.astype(F32) + scale_two * (
        grad_unit - unit_two * jnp.mean(grad_unit * unit_two, axis=-1, keepdims=True)
    )

    branch = seq_gather(grad_middle.astype(BF16))
    grad_attended = dot(out_full, branch, 0, 1).astype(BF16)
    reduced_out = dp_scatter(
        [dot(feature_block(branch, k), attended, 0, 0).astype(BF16) for k in range(planes)]
    )
    grad_query, grad_pair = attention_backward(
        seq_at,
        starts,
        query,
        key,
        key_t,
        value,
        lse,
        grad_attended,
        cosine,
        sine,
        heads,
        share,
        size,
        documents,
    )
    inner = lane % share
    chunks = grad_pair.reshape(share, kept, length)
    pair_sum = lax.dynamic_index_in_dim(chunks, inner, 0, keepdims=False)
    for mask in range(1, share):
        chunk = lax.dynamic_index_in_dim(chunks, inner ^ mask, 0, keepdims=False)
        pair_sum = pair_sum + swap(chunk, mask)
    grad_mixed = jnp.concatenate([grad_query, pair_sum.astype(BF16)], axis=0)

    def own_columns(array):
        pair = lax.dynamic_slice_in_dim(array[:, columns:], inner * kept, kept, 1)
        return jnp.concatenate([array[:, :columns], pair], axis=1)

    reduced_qkv = dp_scatter(
        [dot(feature_block(normed, k), grad_mixed, 0, 1).astype(BF16) for k in range(planes)]
    )
    grad_normed = seq_scatter(dot(grad_mixed, own_columns(qkv_full), 0, 1).astype(BF16))
    unit_one = in_turned.astype(F32)
    scale_own = lax.rsqrt(jnp.mean(unit_one * unit_one, axis=-1, keepdims=True) + rms_eps)
    unit_one = unit_one * scale_own
    grad_unit = grad_normed * gain_pair[0]
    input_grad = grad_middle + scale_own * (
        grad_unit - unit_one * jnp.mean(grad_unit * unit_one, axis=-1, keepdims=True)
    )
    input_grad = turn_columns(input_grad, (planes - plane) % planes)

    gain_two = dp_scatter([gain_two_sum.reshape(planes, 1, block)[k] for k in range(planes)])
    gain_one = jnp.sum(own_columns(own_qkv[:block]).astype(F32) * reduced_qkv, axis=1)[None, :]
    gain_one = gain_one / gain_pair[:1, :block]
    squares = sum(
        jnp.sum(part * part) for part in (reduced_qkv, reduced_out, reduced_gate_up, reduced_down)
    )
    lines = -(-2 * block // 128)
    carried = jnp.concatenate(
        [
            jnp.concatenate([gain_one, gain_two], axis=0).reshape(2 * block // 128, 128),
            jnp.broadcast_to(squares, (8, 128)),
        ],
        axis=0,
    )
    mask = 1
    while mask < lanes:
        carried = carried + swap(carried, mask)
        mask *= 2
    gain_sums = carried[:lines].reshape(2, block)
    squares = carried[lines:] + jnp.sum(gain_sums * gain_sums)
    mask = 1
    while mask < planes:
        squares = squares + lax.ppermute(
            squares, "dp", [(at, at ^ mask) for at in range(planes)]
        )
        mask *= 2
    grad_norm = jnp.sqrt(squares[0, 0])
    factor = jnp.minimum(1.0, clip_limit / grad_norm)

    sent = lax.all_to_all(
        reduced_qkv.astype(BF16).reshape(lanes, owned, columns + kept),
        "seq",
        split_axis=0,
        concat_axis=0,
        tiled=True,
    )
    query_grad = sent[:, :, :columns].transpose(1, 0, 2).reshape(owned, query_width)
    pair_grad = (
        sent[:, :, columns:]
        .reshape(KEY_VALUE_HEADS, share, owned, kept)
        .transpose(2, 0, 1, 3)
        .reshape(owned, KEY_VALUE_HEADS, 2, HEAD_SIZE)
        .transpose(0, 2, 1, 3)
        .reshape(owned, 2 * pair_width)
    )
    qkv_grad = jnp.concatenate([query_grad, pair_grad], axis=1).astype(F32)
    sent = lax.all_to_all(
        reduced_out.astype(BF16).reshape(lanes, owned, columns),
        "seq",
        split_axis=0,
        concat_axis=0,
        tiled=True,
    )
    out_grad = sent.transpose(1, 0, 2).reshape(owned, query_width).T.astype(F32)
    gate_up_grad = reduced_gate_up.reshape(2, units, block).transpose(2, 0, 1)
    gains_grad = lax.dynamic_slice_in_dim(gain_sums, lane * owned, owned, 1)

    reduced = (qkv_grad, out_grad, gate_up_grad, reduced_down, gains_grad)
    clipped = tuple(factor * gradient for gradient in reduced)
    masters = (query_key_value_weight, out_weight, gate_up_weight, down_weight, gains)
    firsts = (first_moment_query_key_value, first_out, first_gate_up, first_down, first_gains)
    seconds = (second_moment_query_key_value, second_out, second_gate_up, second_down, second_gains)
    averages = (average_query_key_value, average_out, average_gate_up, average_down, average_gains)
    results = [
        adam_update(
            masters[slot], clipped[slot], firsts[slot], seconds[slot], averages[slot], rates()[slot]
        )
        for slot in range(5)
    ]
    return (output, input_grad, grad_norm) + clipped + tuple(
        results[slot][part] for part in range(4) for slot in range(5)
    )


def solution(mesh):
    rows = P(("dp", "seq"), None)
    weights = (rows, P(None, ("dp", "seq")), P("dp", None, "seq"), P("seq", "dp"))
    weights = weights + (P(None, ("dp", "seq")),)
    return jax.shard_map(
        on_device,
        mesh=mesh,
        in_specs=(rows, rows, P("dp", None)) + weights * 4,
        out_specs=(rows, rows, P()) + weights * 5,
        check_vma=False,
    )
```

```python
import functools

import jax
import jax.numpy as jnp
from jax import lax
from jax.experimental import pallas as pl
from jax.experimental.pallas import tpu as pltpu
from jax.sharding import PartitionSpec as P

MODEL_WIDTH = 2048
FF = 5632
QUERY_HEAD_COUNT = 32
KEY_VALUE_HEADS = 4
HEAD_SIZE = 64
STEP = 10

rms_eps = 1e-05
rope_base = 10000.0
clip_limit = 1.0
beta_one = 0.9
beta_two = 0.95
adam_eps = 1e-08
weight_decay = 0.1
ema_decay = 0.8
masked_score = -1e30

HALF = HEAD_SIZE // 2
SCALE = HEAD_SIZE ** (-0.5)
F32 = jnp.float32
BF16 = jnp.bfloat16


def dot(left, right, left_dim, right_dim):
    return lax.dot_general(
        left, right, (((left_dim,), (right_dim,)), ((), ())), preferred_element_type=F32
    )


def swap(value, mask):
    count = lax.axis_size("seq")
    return lax.ppermute(value, "seq", [(at, at ^ mask) for at in range(count)])


def seq_order(count):
    return list(range(0, count, 2)) + list(range(1, count, 2))


def assemble_kernel(plan, *refs):
    for k, spans in enumerate(plan):
        at = 0
        for piece, low, high in spans:
            refs[len(refs) - len(plan) + k][at : at + high - low, :] = refs[piece][low:high, :]
            at += high - low


def assemble(pieces, plan=None):
    plan = plan or [[(k, 0, piece.shape[0]) for k, piece in enumerate(pieces)]]
    width, kind = pieces[0].shape[1], pieces[0].dtype
    shapes = [(sum(high - low for _, low, high in spans), width) for spans in plan]
    return pl.pallas_call(
        functools.partial(assemble_kernel, plan),
        out_shape=[jax.ShapeDtypeStruct(shape, kind) for shape in shapes],
        in_specs=[pl.BlockSpec(memory_space=pltpu.VMEM)] * len(pieces),
        out_specs=[pl.BlockSpec(memory_space=pltpu.VMEM)] * len(plan),
        cost_estimate=pl.CostEstimate(
            flops=0,
            bytes_accessed=4 * width * sum(shape[0] for shape in shapes),
            transcendentals=0,
        ),
        name="assemble",
    )(*pieces)


def gather_begin(rows):
    count = lax.axis_size("seq")
    if count != 8:
        return tuple(swap(rows, mask) for mask in range(2, count, 2))
    return swap(rows, 2), swap(rows, 4)


def gather_end(rows, first, *events):
    if lax.axis_size("seq") != 8:
        mine = assemble((rows,) + first)[0]
    else:
        half = rows.shape[0] // 2
        upper, lower = swap(first[0][:half], 4), swap(first[1][half:], 2)
        mine = assemble([rows, first[0], first[1], upper, lower])[0]
    return mine, swap(after(mine, *events) if events else mine, 1)


def seq_gather_two(one, two):
    if lax.axis_size("seq") != 8:
        return tuple(gather_end(rows, gather_begin(rows)) for rows in (one, two))
    size = one.shape[0]
    rows = jnp.concatenate([one, two], axis=0)
    by_x, by_y = swap(rows, 2), swap(rows, 4)
    upper, lower = swap(by_x[:size], 4), swap(by_y[size:], 2)
    plan = [
        [(0, 0, size), (2, 0, size), (3, 0, size), (4, 0, size)],
        [(1, 0, size), (2, size, 2 * size), (3, size, 2 * size), (5, 0, size)],
    ]
    one, two = assemble([one, two, by_x, by_y, upper, lower], plan)
    return (one, swap(one, 1)), (two, swap(two, 1))


class Scatter:
    def __init__(self, mine, other, *events):
        self.mine, self.moved = mine, swap(after(other, *events) if events else other, 1)
        self.count = lax.axis_size("seq")
        self.size = 2 * mine.shape[0] // self.count

    def slot(self, mask, low=0, high=1):
        at, half = (mask // 2) * self.size, self.size // 2
        span = slice(at + low * half, at + high * half)
        return self.mine[span].astype(F32) + self.moved[span].astype(F32)

    def first(self, *events):
        if self.count != 8:
            return (self.moved,)
        slot = self.slot
        by_x = jnp.concatenate([slot(6), slot(2)], axis=0).astype(BF16)
        by_y = jnp.concatenate([slot(6, 1, 2), slot(4, 1, 2)], axis=0).astype(BF16)
        if events:
            by_x, by_y = after(by_x, *events), after(by_y, *events)
        self.by_x, self.by_y = swap(by_x, 2), swap(by_y, 4)
        return self.by_x, self.by_y

    def total(self, *events):
        slot, half = self.slot, self.size // 2
        if self.count != 8:
            total = slot(0, 0, 2)
            for mask in range(2, self.count, 2):
                total = total + swap(slot(mask, 0, 2).astype(BF16), mask).astype(F32)
            return total
        by_x = (slot(2, 1, 2) + self.by_y[:half].astype(F32)).astype(BF16)
        by_y = (slot(4) + self.by_x[:half].astype(F32)).astype(BF16)
        if events:
            by_x, by_y = after(by_x, *events), after(by_y, *events)
        by_x, by_y = swap(by_x, 2), swap(by_y, 4)
        upper = slot(0) + self.by_x[half:].astype(F32) + by_y.astype(F32)
        lower = slot(0, 1, 2) + self.by_y[half:].astype(F32) + by_x.astype(F32)
        return jnp.concatenate([upper, lower], axis=0)


def after(value, *events):
    return lax.optimization_barrier((value,) + events)[0]


def cross(value, mask):
    count = lax.axis_size("dp")
    return lax.ppermute(value, "dp", [(at, at ^ mask) for at in range(count)])


def dp_send(own, other):
    top = lax.axis_size("dp") // 2
    parts = {0: own, top: cross(other, top)}
    if top > 1:
        parts[1] = cross(own, 1)
    return parts


def dp_finish(parts):
    top = lax.axis_size("dp") // 2
    bit = 1
    while bit < top:
        for k in sorted(parts):
            if k ^ bit not in parts:
                parts[k ^ bit] = cross(parts[k], bit)
        bit *= 2
    return [parts[k] for k in range(2 * top)]


def dp_scatter(blocks, *events):
    top = lax.axis_size("dp") // 2
    kind = blocks[0].dtype
    blocks = {k: part for k, part in enumerate(blocks)}
    bit = top // 2
    while bit:
        for k in sorted(blocks, reverse=True):
            if k & bit:
                moved = cross(blocks[k], bit).astype(F32)
                blocks[k ^ bit] = (blocks[k ^ bit].astype(F32) + moved).astype(kind)
                del blocks[k]
        bit //= 2
    last = blocks[top].astype(kind)
    return blocks[0], cross(after(last, *events) if events else last, top)


def reorder_kernel(count, plane_ref, in_ref, out_ref):
    block = in_ref.shape[1] // count
    for k in range(count):
        source = pl.multiple_of(lax.bitwise_xor(plane_ref[0], k) * block, block)
        out_ref[:, k * block : (k + 1) * block] = in_ref[:, pl.ds(source, block)]


def reorder_columns(value):
    plane = lax.axis_index("dp").astype(jnp.int32).reshape(1)
    return pl.pallas_call(
        functools.partial(reorder_kernel, lax.axis_size("dp")),
        out_shape=jax.ShapeDtypeStruct(value.shape, value.dtype),
        in_specs=[pl.BlockSpec(memory_space=pltpu.SMEM), pl.BlockSpec(memory_space=pltpu.VMEM)],
        out_specs=pl.BlockSpec(memory_space=pltpu.VMEM),
        name="reorder",
    )(plane, value)


def output_kernel(count, plane_ref, middle_ref, near_ref, far_ref, out_ref):
    block = middle_ref.shape[1] // count
    for k in range(count):
        at = lax.bitwise_xor(plane_ref[0], k)
        span = pl.ds(pl.multiple_of(at * block, block), block)
        paired = lax.bitwise_xor(at, count // 2)
        far = far_ref[:, pl.ds(pl.multiple_of(paired * block, block), block)].astype(F32)
        total = middle_ref[:, span] + near_ref[:, span] + far
        out_ref[:, k * block : (k + 1) * block] = total.astype(BF16)


def plain_output(middle, near, far):
    plane = lax.axis_index("dp").astype(jnp.int32).reshape(1)
    return pl.pallas_call(
        functools.partial(output_kernel, lax.axis_size("dp")),
        out_shape=jax.ShapeDtypeStruct(middle.shape, BF16),
        in_specs=[pl.BlockSpec(memory_space=pltpu.SMEM)]
        + [pl.BlockSpec(memory_space=pltpu.VMEM)] * 3,
        out_specs=pl.BlockSpec(memory_space=pltpu.VMEM),
        name="plain_output",
    )(plane, middle, near, far)


def swap_halves(value):
    return jnp.roll(value, value.shape[1] // 2, axis=1)


def block_rows(length):
    return min(256, length)


def slot_place(lane, chunk, count, size):
    mask = lax.bitwise_xor(lane, chunk)
    odd = lax.bitwise_and(mask, 1)
    slot = lax.shift_right_logical(mask, 1) + odd * (count // 2)
    return pl.ds(pl.multiple_of(slot * size, size), size)


def slot_span(seq_ref, chunk, count, size):
    return slot_place(seq_ref[0], chunk, count, size)


def allowed_pairs(start_ref, documents, row_from, width, rows):
    key_at = lax.broadcasted_iota(jnp.int32, (width, rows), 0)
    query_at = row_from + lax.broadcasted_iota(jnp.int32, (width, rows), 1)
    allowed = key_at <= query_at
    if documents > 1:
        allowed = allowed & (key_at >= start_ref[:, row_from : row_from + rows])
    return allowed


def forward_kernel(
    heads,
    size,
    documents,
    seq_ref,
    start_ref,
    mixed_ref,
    cos_ref,
    sin_ref,
    out_ref,
    query_ref,
    key_ref,
    key_t_ref,
    value_ref,
    value_t_ref,
    lse_ref,
    gathered,
):
    length = mixed_ref.shape[1]
    width = heads * HEAD_SIZE
    for chunk in range(length // size):
        source = slot_span(seq_ref, chunk, length // size, size)
        place = slice(chunk * size, (chunk + 1) * size)
        cosine, sine = cos_ref[:, place], sin_ref[:, place]
        for head in range(heads + 1):
            base = head * HEAD_SIZE
            one = mixed_ref[base : base + HALF, source]
            two = mixed_ref[base + HALF : base + HEAD_SIZE, source]
            turned = jnp.concatenate(
                [one * cosine - two * sine, two * cosine + one * sine], axis=0
            ).astype(BF16)
            if head < heads:
                query_ref[base : base + HEAD_SIZE, place] = turned
            else:
                key_t_ref[:, place] = turned
        value_t_ref[:, place] = mixed_ref[width + HEAD_SIZE : width + 2 * HEAD_SIZE, source].astype(
            BF16
        )
    key_ref[...] = key_t_ref[...].astype(F32).T.astype(BF16)
    value_ref[...] = value_t_ref[...].astype(F32).T.astype(BF16)
    rows = block_rows(length)
    for block in range(length // rows):
        place = slice(block * rows, (block + 1) * rows)
        reach = (block + 1) * rows
        allowed = allowed_pairs(start_ref, documents, block * rows, reach, rows)
        for head in range(heads):
            span = slice(head * HEAD_SIZE, (head + 1) * HEAD_SIZE)
            query = query_ref[span, place] * jnp.asarray(SCALE, BF16)
            scores = jnp.where(allowed, dot(key_ref[:reach], query, 1, 0), masked_score)
            peak = jnp.max(scores, axis=0, keepdims=True)
            raised = jnp.exp(scores - peak)
            total = jnp.sum(raised, axis=0, keepdims=True)
            lse_ref[head : head + 1, place] = peak + jnp.log(total)
            weights = (raised * (1.0 / total)).astype(BF16)
            gathered[span, :] = dot(value_t_ref[:, :reach], weights, 1, 0)
        out = gathered[...].T.astype(BF16)
        for piece in range(rows // size):
            target = slot_span(
                seq_ref, block * (rows // size) + piece, length // size, size
            )
            out_ref[target, :] = out[piece * size : (piece + 1) * size]


def backward_kernel(
    heads,
    share,
    size,
    documents,
    seq_ref,
    start_ref,
    query_ref,
    key_ref,
    key_t_ref,
    value_ref,
    lse_ref,
    grad_ref,
    cos_ref,
    sin_ref,
    grad_query_ref,
    grad_pair_ref,
    grad_key,
    grad_value,
):
    length = query_ref.shape[1]
    rows = block_rows(length)
    pieces = rows // size
    grad_key[...] = jnp.zeros_like(grad_key)
    grad_value[...] = jnp.zeros_like(grad_value)
    for block in range(length // rows):
        place = slice(block * rows, (block + 1) * rows)
        reach = (block + 1) * rows
        allowed = allowed_pairs(start_ref, documents, block * rows, reach, rows)
        cosine, sine = cos_ref[:, place], sin_ref[:, place]
        spans = [
            slot_span(seq_ref, block * pieces + piece, length // size, size)
            for piece in range(pieces)
        ]
        for head in range(heads):
            base = head * HEAD_SIZE
            span = slice(base, base + HEAD_SIZE)
            query = query_ref[span, place] * jnp.asarray(SCALE, BF16)
            grad = jnp.concatenate([grad_ref[span, where] for where in spans], axis=1)
            scores = jnp.where(allowed, dot(key_ref[:reach], query, 1, 0), masked_score)
            weights = jnp.exp(scores - lse_ref[head : head + 1, place])
            slope = dot(value_ref[:reach], grad, 1, 0)
            delta = jnp.sum(weights * slope, axis=0, keepdims=True)
            inner = (weights * (slope - delta)).astype(BF16)
            pulled = (dot(key_t_ref[:, :reach], inner, 1, 0) * SCALE).astype(BF16).astype(F32)
            one, two = pulled[:HALF], pulled[HALF:]
            turned = jnp.concatenate(
                [one * cosine + two * sine, two * cosine - one * sine], axis=0
            ).astype(BF16)
            for piece, where in enumerate(spans):
                grad_query_ref[span, where] = turned[:, piece * size : (piece + 1) * size]
            grad_key[:reach] += dot(inner, query, 1, 1)
            grad_value[:reach] += dot(weights.astype(BF16), grad, 1, 1)
    key_t = grad_key[...].T
    value_t = grad_value[...].T
    one, two = key_t[:HALF], key_t[HALF:]
    cosine, sine = cos_ref[...], sin_ref[...]
    turned = jnp.concatenate([one * cosine + two * sine, two * cosine - one * sine], axis=0)
    both = jnp.concatenate([turned, value_t], axis=0)
    kept = 2 * HEAD_SIZE // share
    first_sharer = seq_ref[0] - lax.rem(seq_ref[0], share)
    for sharer in range(share):
        span = slice(sharer * kept, (sharer + 1) * kept)
        for chunk in range(length // size):
            target = slot_place(first_sharer + sharer, chunk, length // size, size)
            grad_pair_ref[span, target] = both[span, chunk * size : (chunk + 1) * size]


def weight_kernel(count, parts, *refs):
    left, right = refs[:parts], refs[parts : 2 * parts]
    left_two, right_two = refs[2 * parts : 3 * parts], refs[3 * parts : 4 * parts]
    outs = refs[4 * parts :]
    split = left[0].shape[0]
    one = dot(left[0][...], right[0][...], 1, 0)
    two = dot(left_two[0][...], right_two[0][...], 1, 0)
    for part in range(1, parts):
        one = one + dot(left[part][...], right[part][...], 1, 0)
        two = two + dot(left_two[part][...], right_two[part][...], 1, 0)
    for k in range(count):

        @pl.when(pl.program_id(0) == k)
        def _():
            outs[k][:split, :] = one.astype(BF16)
            outs[k][split:, :] = two.astype(BF16)


def weight_blocks(left, right, left_two, right_two, count):
    rows, depth = left[0].shape
    rows_two = left_two[0].shape[0]
    block = right[0].shape[1] // count
    parts = len(left)

    def specs(height):
        return [pl.BlockSpec((height, depth), lambda k: (0, 0))] * parts + [
            pl.BlockSpec((depth, block), lambda k: (0, k))
        ] * parts

    return pl.pallas_call(
        functools.partial(weight_kernel, count, parts),
        grid=(count,),
        out_shape=[jax.ShapeDtypeStruct((rows + rows_two, block), BF16)] * count,
        in_specs=specs(rows) + specs(rows_two),
        out_specs=[pl.BlockSpec((rows + rows_two, block), lambda k: (0, 0))] * count,
        compiler_params=pltpu.CompilerParams(vmem_limit_bytes=48 << 20),
        cost_estimate=pl.CostEstimate(
            flops=2 * (rows + rows_two) * depth * parts * block * count,
            bytes_accessed=4 * parts * depth * block * count,
            transcendentals=0,
        ),
        name="weight_blocks",
    )(*left, *right, *left_two, *right_two)


def attention_cost(heads, length, dots):
    return pl.CostEstimate(
        flops=dots * heads * length * length * 256,
        bytes_accessed=8 * length * heads * HEAD_SIZE,
        transcendentals=heads * length * length,
    )


def vmem_specs(count):
    return [pl.BlockSpec(memory_space=pltpu.VMEM)] * count


def attention_forward(seq_at, starts, mixed, cosine, sine, heads, size, documents):
    length = mixed.shape[1]
    width = heads * HEAD_SIZE
    shape = jax.ShapeDtypeStruct
    return pl.pallas_call(
        functools.partial(forward_kernel, heads, size, documents),
        out_shape=[
            shape((length, width), BF16),
            shape((width, length), BF16),
            shape((length, HEAD_SIZE), BF16),
            shape((HEAD_SIZE, length), BF16),
            shape((length, HEAD_SIZE), BF16),
            shape((HEAD_SIZE, length), BF16),
            shape((8, length), F32),
        ],
        in_specs=[pl.BlockSpec(memory_space=pltpu.SMEM)] + vmem_specs(4),
        out_specs=vmem_specs(7),
        scratch_shapes=[pltpu.VMEM((width, block_rows(length)), F32)],
        compiler_params=pltpu.CompilerParams(vmem_limit_bytes=40 << 20),
        cost_estimate=attention_cost(heads, length, 2),
        name="attention_forward",
    )(seq_at, starts, mixed, cosine, sine)


def attention_backward(
    seq_at, starts, query, key, key_t, value, lse, grad, cosine, sine, heads, share, size, documents
):
    width, length = query.shape
    shape = jax.ShapeDtypeStruct
    return pl.pallas_call(
        functools.partial(backward_kernel, heads, share, size, documents),
        out_shape=[shape((width, length), BF16), shape((2 * HEAD_SIZE, length), F32)],
        in_specs=[pl.BlockSpec(memory_space=pltpu.SMEM)] + vmem_specs(9),
        out_specs=vmem_specs(2),
        scratch_shapes=[pltpu.VMEM((length, HEAD_SIZE), F32)] * 2,
        compiler_params=pltpu.CompilerParams(vmem_limit_bytes=40 << 20),
        cost_estimate=attention_cost(heads, length, 5),
        name="attention_backward",
    )(seq_at, starts, query, key, key_t, value, lse, grad, cosine, sine)


def rates():
    return (
        0.5 * (2.0 / MODEL_WIDTH) ** 0.5,
        0.5 * (16.0 / (QUERY_HEAD_COUNT * HEAD_SIZE)) ** 0.5,
        0.5 * (1.0 / MODEL_WIDTH) ** 0.5,
        0.5 * (1.0 / FF) ** 0.5,
        0.3,
    )


def adam_update(weight, gradient, moment_one, moment_two, average, rate):
    first_new = beta_one * moment_one + (1.0 - beta_one) * gradient
    second_new = beta_two * moment_two + (1.0 - beta_two) * gradient * gradient
    corrected = (
        first_new
        / (1.0 - beta_one**STEP)
        / (jnp.sqrt(second_new / (1.0 - beta_two**STEP)) + adam_eps)
    )
    weight_new = weight - rate * (corrected + weight_decay * weight)
    average_new = ema_decay * average + (1.0 - ema_decay) * weight_new
    return (weight_new, first_new, second_new, average_new)


def on_device(
    tokens,
    cotangent,
    lengths,
    query_key_value_weight,
    out_weight,
    gate_up_weight,
    down_weight,
    gains,
    first_moment_query_key_value,
    first_out,
    first_gate_up,
    first_down,
    first_gains,
    second_moment_query_key_value,
    second_out,
    second_gate_up,
    second_down,
    second_gains,
    average_query_key_value,
    average_out,
    average_gate_up,
    average_down,
    average_gains,
):
    planes, lanes = lax.axis_size("dp"), lax.axis_size("seq")
    plane, lane = lax.axis_index("dp"), lax.axis_index("seq")
    size, width = tokens.shape
    length = size * lanes
    documents = lengths.shape[1]
    heads = QUERY_HEAD_COUNT // lanes
    columns = heads * HEAD_SIZE
    share = lanes // KEY_VALUE_HEADS
    kept = 2 * HEAD_SIZE // share
    every = columns + 2 * HEAD_SIZE
    owned = query_key_value_weight.shape[0]
    block = owned * lanes
    query_width = QUERY_HEAD_COUNT * HEAD_SIZE
    pair_width = KEY_VALUE_HEADS * HEAD_SIZE
    units = gate_up_weight.shape[2]
    seq_at = lane.astype(jnp.int32).reshape(1)

    qkv_b = query_key_value_weight.astype(BF16)
    query_part = qkv_b[:, :query_width].reshape(owned, lanes, columns)

    def per_device(part):
        part = part.reshape(owned, KEY_VALUE_HEADS, HEAD_SIZE)
        return jnp.repeat(part, share, axis=1)

    key_part = per_device(qkv_b[:, query_width : query_width + pair_width])
    value_part = per_device(qkv_b[:, query_width + pair_width :])
    message = jnp.concatenate([query_part, key_part, value_part], axis=2).transpose(1, 0, 2)
    gain_row = jnp.pad(gains.astype(BF16).reshape(1, 2 * owned), ((0, 7), (0, every - 2 * owned)))
    message = jnp.concatenate(
        [message, jnp.broadcast_to(gain_row[None], (lanes, 8, every))], axis=1
    )
    top = planes // 2
    half = plane // top
    tokens = reorder_columns(after(tokens, message))
    cotangent = reorder_columns(after(cotangent, message))
    grad_far = cross(swap_halves(cotangent), top)

    message = lax.all_to_all(message, "seq", split_axis=0, concat_axis=0, tiled=True)
    own_qkv = after(message[:, :owned].reshape(block, every), grad_far)
    own_qkv = jnp.concatenate([own_qkv, message[:, owned]], axis=0)
    qkv_parts = dp_send(own_qkv, own_qkv)
    qkv_events = list(qkv_parts.values())
    qkv_parts = dp_finish(qkv_parts)
    qkv_full = jnp.concatenate([part[:block] for part in qkv_parts], axis=0)
    gain_pair = jnp.concatenate(
        [
            part[block:, : 2 * owned].reshape(lanes, 2, owned).transpose(1, 0, 2).reshape(2, block)
            for part in qkv_parts
        ],
        axis=1,
    ).astype(F32)

    in_all = gather_end(tokens, gather_begin(tokens))
    grad_near, grad_far = seq_gather_two(cotangent, grad_far)

    out_b = out_weight.T.astype(BF16).reshape(owned, lanes, columns).transpose(1, 0, 2)
    out_b = lax.all_to_all(out_b, "seq", split_axis=0, concat_axis=0, tiled=True)
    out_b = after(out_b.reshape(block, columns), *qkv_events)
    out_parts = dp_send(out_b, out_b)
    out_events = list(out_parts.values())
    out_full = jnp.concatenate(dp_finish(out_parts), axis=0)

    few = units // 2

    def half_of(array, which):
        return lax.dynamic_slice_in_dim(array, which * few, few, array.ndim - 2)

    gate_up_b = gate_up_weight.transpose(1, 2, 0).astype(BF16)
    gate_up_near = half_of(gate_up_b, half).reshape(2 * few, block)
    gate_up_far = half_of(gate_up_b, 1 - half).reshape(2 * few, block)
    gate_up_parts = dp_send(after(gate_up_near, *qkv_events), after(gate_up_far, *qkv_events))
    gate_up_events = list(gate_up_parts.values())
    gate_up_parts = dp_finish(gate_up_parts)
    gate_up_last = gate_up_parts[-1]
    gate_up_full = jnp.concatenate(gate_up_parts, axis=1)
    down_b = down_weight.astype(BF16)
    down_parts = dp_send(
        after(half_of(down_b, half), *gate_up_events),
        after(half_of(down_b, 1 - half), *gate_up_events),
    )
    down_events = list(down_parts.values())
    down_parts = dp_finish(down_parts)
    down_last = down_parts[-1]
    down_full = jnp.concatenate(down_parts, axis=1)

    ends = jnp.cumsum(lengths[0])
    places = jnp.arange(length, dtype=jnp.int32)
    begins = (ends - lengths[0])[None, :]
    within = (places[:, None] >= begins) & (places[:, None] < ends[None, :])
    starts = jnp.sum(jnp.where(within, begins, 0), axis=1).astype(jnp.int32)
    frequency = rope_base ** (-2.0 * jnp.arange(HALF, dtype=F32) / HEAD_SIZE)
    phases = frequency[:, None] * (places - starts).astype(F32)[None, :]
    cosine, sine = jnp.cos(phases), jnp.sin(phases)
    starts = starts[None, :]

    gain_pair = after(gain_pair, grad_near[0], grad_far[0])

    def norm_one(rows):
        rows = rows.astype(F32)
        scale = lax.rsqrt(jnp.mean(rows * rows, axis=-1, keepdims=True) + rms_eps)
        return (rows * scale * gain_pair[0]).astype(BF16)

    normed = jnp.concatenate([norm_one(rows) for rows in in_all], axis=0)
    mixed = after(dot(qkv_full, normed, 0, 1), grad_near[1], grad_far[1])
    attended, query, key, key_t, value, _, lse = attention_forward(
        seq_at, starts, mixed, cosine, sine, heads, size, documents
    )
    side = length // 2

    def halves(array):
        return array[:side], array[side:]

    part = [dot(rows, out_full, 1, 1).astype(BF16) for rows in halves(attended)]
    scatter = Scatter(*part, *gate_up_events)
    scatter.first()
    middle = tokens.astype(F32) + scatter.total(*down_events)

    scale_two = lax.rsqrt(jnp.mean(middle * middle, axis=-1, keepdims=True) + rms_eps)
    unit_two = middle * scale_two
    normed_two = (unit_two * gain_pair[1]).astype(BF16)
    normed_far = cross(swap_halves(normed_two), top)
    near_first = gather_begin(after(normed_two, gate_up_last))
    near_first = lax.optimization_barrier(near_first + (down_last, normed_far))
    normed_far = near_first[-1]
    far_first = gather_begin(normed_far)
    normed_near = gather_end(normed_two, near_first[:-2], *far_first)
    normed_far = gather_end(normed_far, far_first)

    def feed_forward(rows, grads):
        gate_up = dot(gate_up_full, rows, 1, 1)
        gate, up = gate_up[:few], gate_up[few:]
        sigmoid = jax.nn.sigmoid(gate)
        hidden = (gate * sigmoid * up).astype(BF16)
        grad_hidden = dot(down_full, grads, 1, 1)
        grad_gate = grad_hidden * up * sigmoid * (1.0 + gate * (1.0 - sigmoid))
        grad_up = grad_hidden * gate * sigmoid
        grad_gate_up = jnp.concatenate([grad_gate.astype(BF16), grad_up.astype(BF16)], axis=0)
        return hidden, grad_gate_up, dot(grad_gate_up, gate_up_full, 0, 0).astype(BF16)

    rows_in = normed_near + normed_far
    grads_in = grad_near + grad_far
    done = [feed_forward(rows, grads) for rows, grads in zip(rows_in, grads_in)]
    hidden, grad_units, parts = zip(*done)
    scatters = [Scatter(parts[0], parts[1]), Scatter(parts[2], parts[3])]
    scatters[0].first()
    near_sum = scatters[0].total()

    unit_blocks = weight_blocks(
        [after(array, scatters[1].moved) for array in grad_units],
        rows_in,
        [after(array, scatters[1].moved) for array in hidden],
        grads_in,
        planes,
    )

    scatters[1].first()
    far_sum = scatters[1].total()

    def from_far(total):
        return swap_halves(cross(total.astype(BF16), top)).astype(F32)

    out_far = [dot(after(h, far_sum), down_full, 0, 0).astype(BF16) for h in hidden[2:]]
    from_far_sum = from_far(far_sum)
    out_far = Scatter(*out_far, from_far_sum)
    out_far.first()
    unit_blocks = [after(part, far_sum) for part in unit_blocks]

    grad_normed_two = near_sum + from_far_sum
    grad_unit = grad_normed_two * gain_pair[1]
    gain_two_sum = jnp.sum(grad_normed_two * unit_two, axis=0)
    grad_middle = cotangent.astype(F32) + scale_two * (
        grad_unit - unit_two * jnp.mean(grad_unit * unit_two, axis=-1, keepdims=True)
    )
    branch_own = grad_middle.astype(BF16)

    branch = gather_end(branch_own, gather_begin(branch_own))
    grad_attended = jnp.concatenate(
        [dot(out_full, rows, 0, 1).astype(BF16) for rows in branch], axis=1
    )

    out_far = out_far.total(branch[0])
    out_near = [dot(after(h, grad_attended), down_full, 0, 0).astype(BF16) for h in hidden[:2]]
    out_near = Scatter(*out_near)

    grad_query, grad_pair = attention_backward(
        seq_at,
        starts,
        query,
        key,
        key_t,
        value,
        lse,
        grad_attended,
        cosine,
        sine,
        heads,
        share,
        size,
        documents,
    )
    unit_sums = dp_scatter(unit_blocks)
    inner = lane % share
    chunks = grad_pair.reshape(share, kept, length)
    pair_sum = lax.dynamic_index_in_dim(chunks, inner, 0, keepdims=False)
    for mask in range(1, share):
        chunk = lax.dynamic_index_in_dim(chunks, inner ^ mask, 0, keepdims=False)
        pair_sum = pair_sum + swap(chunk, mask)
    grad_mixed = jnp.concatenate([grad_query, pair_sum.astype(BF16)], axis=0)
    grad_mixed = after(grad_mixed, out_far)

    def own_columns(array):
        pair = lax.dynamic_slice_in_dim(array[:, columns:], inner * kept, kept, 1)
        return jnp.concatenate([array[:, :columns], pair], axis=1)

    grad_out_full = sum(dot(rows, part, 0, 0) for rows, part in zip(branch, halves(attended)))
    both_full = jnp.concatenate(
        [grad_out_full.astype(BF16), dot(normed, grad_mixed, 0, 1).astype(BF16)], axis=1
    )
    own_full = own_columns(qkv_full)
    grad_normed = Scatter(
        *[
            dot(part, own_full, 0, 1).astype(BF16)
            for part in (grad_mixed[:, :side], grad_mixed[:, side:])
        ]
    )
    first = grad_normed.first()
    out_near.first(*first)
    both = dp_scatter([both_full[k * block : (k + 1) * block] for k in range(planes)], *first)
    out_far = after(cross(out_far.astype(BF16), top), both[1])
    output = plain_output(middle, out_near.total(), out_far)
    both = both[0].astype(F32) + both[1].astype(F32)
    reduced_out, reduced_qkv = both[:, :columns], both[:, columns:]
    grad_normed = grad_normed.total()
    unit_sums = [after(part, both_full) for part in unit_sums]

    def whole_units(low, high):
        pair = [part[low:high].astype(F32) for part in unit_sums]
        return jnp.where(
            half == 0, jnp.concatenate(pair, axis=0), jnp.concatenate(pair[::-1], axis=0)
        )

    reduced_gate_up = jnp.stack([whole_units(0, few), whole_units(few, 2 * few)])
    reduced_down = whole_units(2 * few, 3 * few)
    unit_one = tokens.astype(F32)
    scale_own = lax.rsqrt(jnp.mean(unit_one * unit_one, axis=-1, keepdims=True) + rms_eps)
    unit_one = unit_one * scale_own
    grad_unit = grad_normed * gain_pair[0]
    input_grad = grad_middle + scale_own * (
        grad_unit - unit_one * jnp.mean(grad_unit * unit_one, axis=-1, keepdims=True)
    )
    input_grad = reorder_columns(input_grad)

    gain_one = jnp.sum(own_columns(own_qkv[:block]).astype(F32) * reduced_qkv, axis=1)
    gain_one = (gain_one / gain_pair[0, :block]).reshape(block // 128, 128)
    gain_two_sum = reorder_columns(jnp.broadcast_to(gain_two_sum, (8, width)))[0]
    squares = sum(
        jnp.sum(part * part) for part in (reduced_qkv, reduced_out, reduced_gate_up, reduced_down)
    )
    carried = jnp.concatenate(
        [
            gain_two_sum.reshape(width // 128, 128),
            jnp.broadcast_to(squares, (8, 128)),
            gain_one,
        ],
        axis=0,
    )
    carried = after(carried, output, input_grad)
    mask = 1
    while mask < lanes:
        carried = carried + swap(carried, mask)
        mask *= 2
    lines = width // 128
    gain_one = carried[lines + 8 :]
    carried = jnp.concatenate(
        [carried[:lines], carried[lines : lines + 8] + jnp.sum(gain_one * gain_one)], axis=0
    )
    mask = 1
    while mask < planes:
        carried = carried + lax.ppermute(
            carried, "dp", [(at, at ^ mask) for at in range(planes)]
        )
        mask *= 2
    gain_two = carried[:lines]
    squares = carried[lines:] + jnp.sum(gain_two * gain_two)
    grad_norm = jnp.sqrt(squares[0, 0])
    factor = jnp.minimum(1.0, clip_limit / grad_norm)

    sent = lax.all_to_all(
        both.astype(BF16).reshape(lanes, owned, 2 * columns + kept),
        "seq",
        split_axis=0,
        concat_axis=0,
        tiled=True,
    )
    out_grad = sent[:, :, :columns].transpose(1, 0, 2).reshape(owned, query_width).T.astype(F32)
    sent = sent[:, :, columns:]
    query_grad = sent[:, :, :columns].transpose(1, 0, 2).reshape(owned, query_width)
    pair_grad = (
        sent[:, :, columns:]
        .reshape(KEY_VALUE_HEADS, share, owned, kept)
        .transpose(2, 0, 1, 3)
        .reshape(owned, KEY_VALUE_HEADS, 2, HEAD_SIZE)
        .transpose(0, 2, 1, 3)
        .reshape(owned, 2 * pair_width)
    )
    qkv_grad = jnp.concatenate([query_grad, pair_grad], axis=1).astype(F32)
    gate_up_grad = reduced_gate_up.transpose(2, 0, 1)
    gains_grad = jnp.stack(
        [
            lax.dynamic_slice_in_dim(gain_one.reshape(block), lane * owned, owned, 0),
            lax.dynamic_slice_in_dim(
                gain_two.reshape(width), (plane * lanes + lane) * owned, owned, 0
            ),
        ]
    )

    reduced = (qkv_grad, out_grad, gate_up_grad, reduced_down, gains_grad)
    clipped = tuple(factor * gradient for gradient in reduced)
    masters = (query_key_value_weight, out_weight, gate_up_weight, down_weight, gains)
    firsts = (first_moment_query_key_value, first_out, first_gate_up, first_down, first_gains)
    seconds = (second_moment_query_key_value, second_out, second_gate_up, second_down, second_gains)
    averages = (average_query_key_value, average_out, average_gate_up, average_down, average_gains)
    results = [
        adam_update(
            masters[slot], clipped[slot], firsts[slot], seconds[slot], averages[slot], rates()[slot]
        )
        for slot in range(5)
    ]
    return (output, input_grad, grad_norm) + clipped + tuple(
        results[slot][part] for part in range(4) for slot in range(5)
    )


def solution(mesh):
    rows = P(("dp", "seq"), None)
    weights = (rows, P(None, ("dp", "seq")), P("dp", None, "seq"), P("seq", "dp"))
    weights = weights + (P(None, ("dp", "seq")),)
    return jax.shard_map(
        on_device,
        mesh=mesh,
        in_specs=(rows, rows, P("dp", None)) + weights * 4,
        out_specs=(rows, rows, P()) + weights * 5,
        check_vma=False,
    )
```

```python
import functools

import jax
import jax.numpy as jnp
from jax import lax
from jax.experimental import pallas as pl
from jax.experimental.pallas import tpu as pltpu
from jax.sharding import PartitionSpec as P

MODEL_WIDTH = 2048
FF = 5632
QUERY_HEAD_COUNT = 32
KEY_VALUE_HEADS = 4
HEAD_SIZE = 64
STEP = 10

rms_eps = 1e-05
rope_base = 10000.0
clip_limit = 1.0
beta_one = 0.9
beta_two = 0.95
adam_eps = 1e-08
weight_decay = 0.1
ema_decay = 0.8
masked_score = -1e30

HALF = HEAD_SIZE // 2
SCALE = HEAD_SIZE ** (-0.5)
F32 = jnp.float32
BF16 = jnp.bfloat16


def dot(left, right, left_dim, right_dim):
    return lax.dot_general(
        left, right, (((left_dim,), (right_dim,)), ((), ())), preferred_element_type=F32
    )


def swap(value, mask):
    count = lax.axis_size("seq")
    return lax.ppermute(value, "seq", [(at, at ^ mask) for at in range(count)])


def seq_order(count):
    return list(range(0, count, 2)) + list(range(1, count, 2))


def assemble_kernel(plan, *refs):
    for k, spans in enumerate(plan):
        at = 0
        for piece, low, high in spans:
            refs[len(refs) - len(plan) + k][at : at + high - low, :] = refs[piece][low:high, :]
            at += high - low


def assemble(pieces, plan=None):
    plan = plan or [[(k, 0, piece.shape[0]) for k, piece in enumerate(pieces)]]
    width, kind = pieces[0].shape[1], pieces[0].dtype
    shapes = [(sum(high - low for _, low, high in spans), width) for spans in plan]
    return pl.pallas_call(
        functools.partial(assemble_kernel, plan),
        out_shape=[jax.ShapeDtypeStruct(shape, kind) for shape in shapes],
        in_specs=[pl.BlockSpec(memory_space=pltpu.VMEM)] * len(pieces),
        out_specs=[pl.BlockSpec(memory_space=pltpu.VMEM)] * len(plan),
        cost_estimate=pl.CostEstimate(
            flops=0,
            bytes_accessed=4 * width * sum(shape[0] for shape in shapes),
            transcendentals=0,
        ),
        name="assemble",
    )(*pieces)


def gather_begin(rows):
    count = lax.axis_size("seq")
    if count != 8:
        return tuple(swap(rows, mask) for mask in range(2, count, 2))
    return swap(rows, 2), swap(rows, 4)


def gather_end(rows, first, *events):
    if lax.axis_size("seq") != 8:
        mine = assemble((rows,) + first)[0]
    else:
        half = rows.shape[0] // 2
        upper, lower = swap(first[0][:half], 4), swap(first[1][half:], 2)
        mine = assemble([rows, first[0], first[1], upper, lower])[0]
    return mine, swap(after(mine, *events) if events else mine, 1)


def seq_gather_two(one, two):
    if lax.axis_size("seq") != 8:
        return tuple(gather_end(rows, gather_begin(rows)) for rows in (one, two))
    size = one.shape[0]
    rows = jnp.concatenate([one, two], axis=0)
    by_x, by_y = swap(rows, 2), swap(rows, 4)
    upper, lower = swap(by_x[:size], 4), swap(by_y[size:], 2)
    plan = [
        [(0, 0, size), (2, 0, size), (3, 0, size), (4, 0, size)],
        [(1, 0, size), (2, size, 2 * size), (3, size, 2 * size), (5, 0, size)],
    ]
    one, two = assemble([one, two, by_x, by_y, upper, lower], plan)
    return (one, swap(one, 1)), (two, swap(two, 1))


class Scatter:
    def __init__(self, mine, other, *events):
        self.mine, self.moved = mine, swap(after(other, *events) if events else other, 1)
        self.count = lax.axis_size("seq")
        self.size = 2 * mine.shape[0] // self.count

    def slot(self, mask, low=0, high=1):
        at, half = (mask // 2) * self.size, self.size // 2
        span = slice(at + low * half, at + high * half)
        return self.mine[span].astype(F32) + self.moved[span].astype(F32)

    def first(self, *events):
        if self.count != 8:
            return (self.moved,)
        slot = self.slot
        by_x = jnp.concatenate([slot(6), slot(2)], axis=0).astype(BF16)
        by_y = jnp.concatenate([slot(6, 1, 2), slot(4, 1, 2)], axis=0).astype(BF16)
        if events:
            by_x, by_y = after(by_x, *events), after(by_y, *events)
        self.by_x, self.by_y = swap(by_x, 2), swap(by_y, 4)
        return self.by_x, self.by_y

    def total(self, *events):
        slot, half = self.slot, self.size // 2
        if self.count != 8:
            total = slot(0, 0, 2)
            for mask in range(2, self.count, 2):
                total = total + swap(slot(mask, 0, 2).astype(BF16), mask).astype(F32)
            return total
        by_x = (slot(2, 1, 2) + self.by_y[:half].astype(F32)).astype(BF16)
        by_y = (slot(4) + self.by_x[:half].astype(F32)).astype(BF16)
        if events:
            by_x, by_y = after(by_x, *events), after(by_y, *events)
        by_x, by_y = swap(by_x, 2), swap(by_y, 4)
        upper = slot(0) + self.by_x[half:].astype(F32) + by_y.astype(F32)
        lower = slot(0, 1, 2) + self.by_y[half:].astype(F32) + by_x.astype(F32)
        return jnp.concatenate([upper, lower], axis=0)


def after(value, *events):
    return lax.optimization_barrier((value,) + events)[0]


def cross(value, mask):
    count = lax.axis_size("dp")
    return lax.ppermute(value, "dp", [(at, at ^ mask) for at in range(count)])


def dp_send(own, other):
    top = lax.axis_size("dp") // 2
    parts = {0: own, top: cross(other, top)}
    if top > 1:
        parts[1] = cross(own, 1)
    return parts


def dp_finish(parts):
    top = lax.axis_size("dp") // 2
    bit = 1
    while bit < top:
        for k in sorted(parts):
            if k ^ bit not in parts:
                parts[k ^ bit] = cross(parts[k], bit)
        bit *= 2
    return [parts[k] for k in range(2 * top)]


def dp_scatter(blocks, *events):
    top = lax.axis_size("dp") // 2
    kind = blocks[0].dtype
    blocks = {k: part for k, part in enumerate(blocks)}
    bit = top // 2
    while bit:
        for k in sorted(blocks, reverse=True):
            if k & bit:
                moved = cross(blocks[k], bit).astype(F32)
                blocks[k ^ bit] = (blocks[k ^ bit].astype(F32) + moved).astype(kind)
                del blocks[k]
        bit //= 2
    last = blocks[top].astype(kind)
    return blocks[0], cross(after(last, *events) if events else last, top)


def reorder_kernel(count, plane_ref, in_ref, out_ref):
    block = in_ref.shape[1] // count
    for k in range(count):
        source = pl.multiple_of(lax.bitwise_xor(plane_ref[0], k) * block, block)
        out_ref[:, k * block : (k + 1) * block] = in_ref[:, pl.ds(source, block)]


def reorder_columns(value):
    plane = lax.axis_index("dp").astype(jnp.int32).reshape(1)
    return pl.pallas_call(
        functools.partial(reorder_kernel, lax.axis_size("dp")),
        out_shape=jax.ShapeDtypeStruct(value.shape, value.dtype),
        in_specs=[pl.BlockSpec(memory_space=pltpu.SMEM), pl.BlockSpec(memory_space=pltpu.VMEM)],
        out_specs=pl.BlockSpec(memory_space=pltpu.VMEM),
        name="reorder",
    )(plane, value)


def output_kernel(count, plane_ref, middle_ref, near_ref, far_ref, out_ref):
    block = middle_ref.shape[1] // count
    for k in range(count):
        at = lax.bitwise_xor(plane_ref[0], k)
        span = pl.ds(pl.multiple_of(at * block, block), block)
        paired = lax.bitwise_xor(at, count // 2)
        far = far_ref[:, pl.ds(pl.multiple_of(paired * block, block), block)].astype(F32)
        total = middle_ref[:, span] + near_ref[:, span] + far
        out_ref[:, k * block : (k + 1) * block] = total.astype(BF16)


def plain_output(middle, near, far):
    plane = lax.axis_index("dp").astype(jnp.int32).reshape(1)
    return pl.pallas_call(
        functools.partial(output_kernel, lax.axis_size("dp")),
        out_shape=jax.ShapeDtypeStruct(middle.shape, BF16),
        in_specs=[pl.BlockSpec(memory_space=pltpu.SMEM)]
        + [pl.BlockSpec(memory_space=pltpu.VMEM)] * 3,
        out_specs=pl.BlockSpec(memory_space=pltpu.VMEM),
        name="plain_output",
    )(plane, middle, near, far)


def swap_halves(value):
    return jnp.roll(value, value.shape[1] // 2, axis=1)


def block_rows(length):
    return min(256, length)


def slot_place(lane, chunk, count, size):
    mask = lax.bitwise_xor(lane, chunk)
    odd = lax.bitwise_and(mask, 1)
    slot = lax.shift_right_logical(mask, 1) + odd * (count // 2)
    return pl.ds(pl.multiple_of(slot * size, size), size)


def slot_span(seq_ref, chunk, count, size):
    return slot_place(seq_ref[0], chunk, count, size)


def allowed_pairs(start_ref, documents, row_from, width, rows):
    key_at = lax.broadcasted_iota(jnp.int32, (width, rows), 0)
    query_at = row_from + lax.broadcasted_iota(jnp.int32, (width, rows), 1)
    allowed = key_at <= query_at
    if documents > 1:
        allowed = allowed & (key_at >= start_ref[:, row_from : row_from + rows])
    return allowed


def forward_kernel(
    heads,
    size,
    documents,
    seq_ref,
    start_ref,
    mixed_ref,
    cos_ref,
    sin_ref,
    out_ref,
    query_ref,
    key_ref,
    key_t_ref,
    value_ref,
    value_t_ref,
    lse_ref,
    gathered,
):
    length = mixed_ref.shape[1]
    width = heads * HEAD_SIZE
    for chunk in range(length // size):
        source = slot_span(seq_ref, chunk, length // size, size)
        place = slice(chunk * size, (chunk + 1) * size)
        cosine, sine = cos_ref[:, place], sin_ref[:, place]
        for head in range(heads + 1):
            base = head * HEAD_SIZE
            one = mixed_ref[base : base + HALF, source]
            two = mixed_ref[base + HALF : base + HEAD_SIZE, source]
            turned = jnp.concatenate(
                [one * cosine - two * sine, two * cosine + one * sine], axis=0
            ).astype(BF16)
            if head < heads:
                query_ref[base : base + HEAD_SIZE, place] = turned
            else:
                key_t_ref[:, place] = turned
        value_t_ref[:, place] = mixed_ref[width + HEAD_SIZE : width + 2 * HEAD_SIZE, source].astype(
            BF16
        )
    key_ref[...] = key_t_ref[...].astype(F32).T.astype(BF16)
    value_ref[...] = value_t_ref[...].astype(F32).T.astype(BF16)
    rows = block_rows(length)
    for block in range(length // rows):
        place = slice(block * rows, (block + 1) * rows)
        reach = (block + 1) * rows
        allowed = allowed_pairs(start_ref, documents, block * rows, reach, rows)
        for head in range(heads):
            span = slice(head * HEAD_SIZE, (head + 1) * HEAD_SIZE)
            query = query_ref[span, place] * jnp.asarray(SCALE, BF16)
            scores = jnp.where(allowed, dot(key_ref[:reach], query, 1, 0), masked_score)
            peak = jnp.max(scores, axis=0, keepdims=True)
            raised = jnp.exp(scores - peak)
            total = jnp.sum(raised, axis=0, keepdims=True)
            lse_ref[head : head + 1, place] = peak + jnp.log(total)
            weights = (raised * (1.0 / total)).astype(BF16)
            gathered[span, :] = dot(value_t_ref[:, :reach], weights, 1, 0)
        out = gathered[...].T.astype(BF16)
        for piece in range(rows // size):
            target = slot_span(
                seq_ref, block * (rows // size) + piece, length // size, size
            )
            out_ref[target, :] = out[piece * size : (piece + 1) * size]


def backward_kernel(
    heads,
    share,
    size,
    documents,
    seq_ref,
    start_ref,
    query_ref,
    key_ref,
    key_t_ref,
    value_ref,
    lse_ref,
    grad_ref,
    cos_ref,
    sin_ref,
    grad_query_ref,
    grad_pair_ref,
    grad_key,
    grad_value,
):
    length = query_ref.shape[1]
    rows = block_rows(length)
    pieces = rows // size
    grad_key[...] = jnp.zeros_like(grad_key)
    grad_value[...] = jnp.zeros_like(grad_value)
    for block in range(length // rows):
        place = slice(block * rows, (block + 1) * rows)
        reach = (block + 1) * rows
        allowed = allowed_pairs(start_ref, documents, block * rows, reach, rows)
        cosine, sine = cos_ref[:, place], sin_ref[:, place]
        spans = [
            slot_span(seq_ref, block * pieces + piece, length // size, size)
            for piece in range(pieces)
        ]
        for head in range(heads):
            base = head * HEAD_SIZE
            span = slice(base, base + HEAD_SIZE)
            query = query_ref[span, place] * jnp.asarray(SCALE, BF16)
            grad = jnp.concatenate([grad_ref[span, where] for where in spans], axis=1)
            scores = jnp.where(allowed, dot(key_ref[:reach], query, 1, 0), masked_score)
            weights = jnp.exp(scores - lse_ref[head : head + 1, place])
            slope = dot(value_ref[:reach], grad, 1, 0)
            delta = jnp.sum(weights * slope, axis=0, keepdims=True)
            inner = (weights * (slope - delta)).astype(BF16)
            pulled = (dot(key_t_ref[:, :reach], inner, 1, 0) * SCALE).astype(BF16).astype(F32)
            one, two = pulled[:HALF], pulled[HALF:]
            turned = jnp.concatenate(
                [one * cosine + two * sine, two * cosine - one * sine], axis=0
            ).astype(BF16)
            for piece, where in enumerate(spans):
                grad_query_ref[span, where] = turned[:, piece * size : (piece + 1) * size]
            grad_key[:reach] += dot(inner, query, 1, 1)
            grad_value[:reach] += dot(weights.astype(BF16), grad, 1, 1)
    key_t = grad_key[...].T
    value_t = grad_value[...].T
    one, two = key_t[:HALF], key_t[HALF:]
    cosine, sine = cos_ref[...], sin_ref[...]
    turned = jnp.concatenate([one * cosine + two * sine, two * cosine - one * sine], axis=0)
    both = jnp.concatenate([turned, value_t], axis=0)
    kept = 2 * HEAD_SIZE // share
    first_sharer = seq_ref[0] - lax.rem(seq_ref[0], share)
    for sharer in range(share):
        span = slice(sharer * kept, (sharer + 1) * kept)
        for chunk in range(length // size):
            target = slot_place(first_sharer + sharer, chunk, length // size, size)
            grad_pair_ref[span, target] = both[span, chunk * size : (chunk + 1) * size]


def weight_kernel(count, parts, *refs):
    left, right = refs[:parts], refs[parts : 2 * parts]
    left_two, right_two = refs[2 * parts : 3 * parts], refs[3 * parts : 4 * parts]
    outs = refs[4 * parts :]
    split = left[0].shape[0]
    one = dot(left[0][...], right[0][...], 1, 0)
    two = dot(left_two[0][...], right_two[0][...], 1, 0)
    for part in range(1, parts):
        one = one + dot(left[part][...], right[part][...], 1, 0)
        two = two + dot(left_two[part][...], right_two[part][...], 1, 0)
    for k in range(count):

        @pl.when(pl.program_id(0) == k)
        def _():
            outs[k][:split, :] = one.astype(BF16)
            outs[k][split:, :] = two.astype(BF16)


def weight_blocks(left, right, left_two, right_two, count):
    rows, depth = left[0].shape
    rows_two = left_two[0].shape[0]
    block = right[0].shape[1] // count
    parts = len(left)

    def specs(height):
        return [pl.BlockSpec((height, depth), lambda k: (0, 0))] * parts + [
            pl.BlockSpec((depth, block), lambda k: (0, k))
        ] * parts

    return pl.pallas_call(
        functools.partial(weight_kernel, count, parts),
        grid=(count,),
        out_shape=[jax.ShapeDtypeStruct((rows + rows_two, block), BF16)] * count,
        in_specs=specs(rows) + specs(rows_two),
        out_specs=[pl.BlockSpec((rows + rows_two, block), lambda k: (0, 0))] * count,
        compiler_params=pltpu.CompilerParams(vmem_limit_bytes=48 << 20),
        cost_estimate=pl.CostEstimate(
            flops=2 * (rows + rows_two) * depth * parts * block * count,
            bytes_accessed=4 * parts * depth * block * count,
            transcendentals=0,
        ),
        name="weight_blocks",
    )(*left, *right, *left_two, *right_two)


def attention_cost(heads, length, dots):
    return pl.CostEstimate(
        flops=dots * heads * length * length * 256,
        bytes_accessed=8 * length * heads * HEAD_SIZE,
        transcendentals=heads * length * length,
    )


def vmem_specs(count):
    return [pl.BlockSpec(memory_space=pltpu.VMEM)] * count


def attention_forward(seq_at, starts, mixed, cosine, sine, heads, size, documents):
    length = mixed.shape[1]
    width = heads * HEAD_SIZE
    shape = jax.ShapeDtypeStruct
    return pl.pallas_call(
        functools.partial(forward_kernel, heads, size, documents),
        out_shape=[
            shape((length, width), BF16),
            shape((width, length), BF16),
            shape((length, HEAD_SIZE), BF16),
            shape((HEAD_SIZE, length), BF16),
            shape((length, HEAD_SIZE), BF16),
            shape((HEAD_SIZE, length), BF16),
            shape((8, length), F32),
        ],
        in_specs=[pl.BlockSpec(memory_space=pltpu.SMEM)] + vmem_specs(4),
        out_specs=vmem_specs(7),
        scratch_shapes=[pltpu.VMEM((width, block_rows(length)), F32)],
        compiler_params=pltpu.CompilerParams(vmem_limit_bytes=40 << 20),
        cost_estimate=attention_cost(heads, length, 2),
        name="attention_forward",
    )(seq_at, starts, mixed, cosine, sine)


def attention_backward(
    seq_at, starts, query, key, key_t, value, lse, grad, cosine, sine, heads, share, size, documents
):
    width, length = query.shape
    shape = jax.ShapeDtypeStruct
    return pl.pallas_call(
        functools.partial(backward_kernel, heads, share, size, documents),
        out_shape=[shape((width, length), BF16), shape((2 * HEAD_SIZE, length), F32)],
        in_specs=[pl.BlockSpec(memory_space=pltpu.SMEM)] + vmem_specs(9),
        out_specs=vmem_specs(2),
        scratch_shapes=[pltpu.VMEM((length, HEAD_SIZE), F32)] * 2,
        compiler_params=pltpu.CompilerParams(vmem_limit_bytes=40 << 20),
        cost_estimate=attention_cost(heads, length, 5),
        name="attention_backward",
    )(seq_at, starts, query, key, key_t, value, lse, grad, cosine, sine)


def rates():
    return (
        0.5 * (2.0 / MODEL_WIDTH) ** 0.5,
        0.5 * (16.0 / (QUERY_HEAD_COUNT * HEAD_SIZE)) ** 0.5,
        0.5 * (1.0 / MODEL_WIDTH) ** 0.5,
        0.5 * (1.0 / FF) ** 0.5,
        0.3,
    )


def adam_update(weight, gradient, moment_one, moment_two, average, rate):
    first_new = beta_one * moment_one + (1.0 - beta_one) * gradient
    second_new = beta_two * moment_two + (1.0 - beta_two) * gradient * gradient
    corrected = (
        first_new
        / (1.0 - beta_one**STEP)
        / (jnp.sqrt(second_new / (1.0 - beta_two**STEP)) + adam_eps)
    )
    weight_new = weight - rate * (corrected + weight_decay * weight)
    average_new = ema_decay * average + (1.0 - ema_decay) * weight_new
    return (weight_new, first_new, second_new, average_new)


def on_device(
    tokens,
    cotangent,
    lengths,
    query_key_value_weight,
    out_weight,
    gate_up_weight,
    down_weight,
    gains,
    first_moment_query_key_value,
    first_out,
    first_gate_up,
    first_down,
    first_gains,
    second_moment_query_key_value,
    second_out,
    second_gate_up,
    second_down,
    second_gains,
    average_query_key_value,
    average_out,
    average_gate_up,
    average_down,
    average_gains,
):
    planes, lanes = lax.axis_size("dp"), lax.axis_size("seq")
    plane, lane = lax.axis_index("dp"), lax.axis_index("seq")
    size, width = tokens.shape
    length = size * lanes
    documents = lengths.shape[1]
    heads = QUERY_HEAD_COUNT // lanes
    columns = heads * HEAD_SIZE
    share = lanes // KEY_VALUE_HEADS
    kept = 2 * HEAD_SIZE // share
    every = columns + 2 * HEAD_SIZE
    owned = query_key_value_weight.shape[0]
    block = owned * lanes
    query_width = QUERY_HEAD_COUNT * HEAD_SIZE
    pair_width = KEY_VALUE_HEADS * HEAD_SIZE
    units = gate_up_weight.shape[2]
    seq_at = lane.astype(jnp.int32).reshape(1)

    qkv_b = query_key_value_weight.astype(BF16)
    query_part = qkv_b[:, :query_width].reshape(owned, lanes, columns)

    def per_device(part):
        part = part.reshape(owned, KEY_VALUE_HEADS, HEAD_SIZE)
        return jnp.repeat(part, share, axis=1)

    key_part = per_device(qkv_b[:, query_width : query_width + pair_width])
    value_part = per_device(qkv_b[:, query_width + pair_width :])
    message = jnp.concatenate([query_part, key_part, value_part], axis=2).transpose(1, 0, 2)
    gain_row = jnp.pad(gains.astype(BF16).reshape(1, 2 * owned), ((0, 7), (0, every - 2 * owned)))
    message = jnp.concatenate(
        [message, jnp.broadcast_to(gain_row[None], (lanes, 8, every))], axis=1
    )
    top = planes // 2
    half = plane // top
    tokens = reorder_columns(after(tokens, message))
    cotangent = reorder_columns(after(cotangent, message))
    grad_far = cross(swap_halves(cotangent), top)

    message = lax.all_to_all(message, "seq", split_axis=0, concat_axis=0, tiled=True)
    own_qkv = after(message[:, :owned].reshape(block, every), grad_far)
    own_qkv = jnp.concatenate([own_qkv, message[:, owned]], axis=0)
    qkv_parts = dp_send(own_qkv, own_qkv)
    qkv_events = list(qkv_parts.values())
    qkv_parts = dp_finish(qkv_parts)
    qkv_full = jnp.concatenate([part[:block] for part in qkv_parts], axis=0)
    gain_pair = jnp.concatenate(
        [
            part[block:, : 2 * owned].reshape(lanes, 2, owned).transpose(1, 0, 2).reshape(2, block)
            for part in qkv_parts
        ],
        axis=1,
    ).astype(F32)

    in_all = gather_end(tokens, gather_begin(tokens))
    grad_near, grad_far = seq_gather_two(cotangent, grad_far)

    out_b = out_weight.T.astype(BF16).reshape(owned, lanes, columns).transpose(1, 0, 2)
    out_b = lax.all_to_all(out_b, "seq", split_axis=0, concat_axis=0, tiled=True)
    out_b = after(out_b.reshape(block, columns), *qkv_events)
    out_parts = dp_send(out_b, out_b)
    out_events = list(out_parts.values())
    out_full = jnp.concatenate(dp_finish(out_parts), axis=0)

    few = units // 2

    def half_of(array, which):
        return lax.dynamic_slice_in_dim(array, which * few, few, array.ndim - 2)

    gate_up_b = gate_up_weight.transpose(1, 2, 0).astype(BF16)
    gate_up_near = half_of(gate_up_b, half).reshape(2 * few, block)
    gate_up_far = half_of(gate_up_b, 1 - half).reshape(2 * few, block)
    gate_up_parts = dp_send(after(gate_up_near, *qkv_events), after(gate_up_far, *qkv_events))
    gate_up_events = list(gate_up_parts.values())
    gate_up_parts = dp_finish(gate_up_parts)
    gate_up_last = gate_up_parts[-1]
    gate_up_full = jnp.concatenate(gate_up_parts, axis=1)
    down_b = down_weight.astype(BF16)
    down_parts = dp_send(
        after(half_of(down_b, half), *gate_up_events),
        after(half_of(down_b, 1 - half), *gate_up_events),
    )
    down_events = list(down_parts.values())
    down_parts = dp_finish(down_parts)
    down_last = down_parts[-1]
    down_full = jnp.concatenate(down_parts, axis=1)

    ends = jnp.cumsum(lengths[0])
    places = jnp.arange(length, dtype=jnp.int32)
    begins = (ends - lengths[0])[None, :]
    within = (places[:, None] >= begins) & (places[:, None] < ends[None, :])
    starts = jnp.sum(jnp.where(within, begins, 0), axis=1).astype(jnp.int32)
    frequency = rope_base ** (-2.0 * jnp.arange(HALF, dtype=F32) / HEAD_SIZE)
    phases = frequency[:, None] * (places - starts).astype(F32)[None, :]
    cosine, sine = jnp.cos(phases), jnp.sin(phases)
    starts = starts[None, :]

    gain_pair = after(gain_pair, grad_near[0], grad_far[0])

    def norm_one(rows):
        rows = rows.astype(F32)
        scale = lax.rsqrt(jnp.mean(rows * rows, axis=-1, keepdims=True) + rms_eps)
        return (rows * scale * gain_pair[0]).astype(BF16)

    normed = jnp.concatenate([norm_one(rows) for rows in in_all], axis=0)
    mixed = after(dot(qkv_full, normed, 0, 1), grad_near[1], grad_far[1])
    attended, query, key, key_t, value, _, lse = attention_forward(
        seq_at, starts, mixed, cosine, sine, heads, size, documents
    )
    side = length // 2

    def halves(array):
        return array[:side], array[side:]

    part = [dot(rows, out_full, 1, 1).astype(BF16) for rows in halves(attended)]
    scatter = Scatter(*part, *gate_up_events)
    scatter.first()
    middle = tokens.astype(F32) + scatter.total(*down_events)

    scale_two = lax.rsqrt(jnp.mean(middle * middle, axis=-1, keepdims=True) + rms_eps)
    unit_two = middle * scale_two
    normed_two = (unit_two * gain_pair[1]).astype(BF16)
    normed_far = cross(swap_halves(normed_two), top)
    near_first = gather_begin(after(normed_two, gate_up_last))
    near_first = lax.optimization_barrier(near_first + (down_last, normed_far))
    normed_far = near_first[-1]
    far_first = gather_begin(normed_far)
    normed_near = gather_end(normed_two, near_first[:-2], *far_first)
    normed_far = gather_end(normed_far, far_first)

    def feed_forward(rows, grads):
        gate_up = dot(gate_up_full, rows, 1, 1)
        gate, up = gate_up[:few], gate_up[few:]
        sigmoid = jax.nn.sigmoid(gate)
        hidden = (gate * sigmoid * up).astype(BF16)
        grad_hidden = dot(down_full, grads, 1, 1)
        grad_gate = grad_hidden * up * sigmoid * (1.0 + gate * (1.0 - sigmoid))
        grad_up = grad_hidden * gate * sigmoid
        grad_gate_up = jnp.concatenate([grad_gate.astype(BF16), grad_up.astype(BF16)], axis=0)
        return hidden, grad_gate_up, dot(grad_gate_up, gate_up_full, 0, 0).astype(BF16)

    rows_in = normed_near + normed_far
    grads_in = grad_near + grad_far
    done = [feed_forward(rows, grads) for rows, grads in zip(rows_in, grads_in)]
    hidden, grad_units, parts = zip(*done)
    scatters = [Scatter(parts[0], parts[1]), Scatter(parts[2], parts[3])]

    unit_blocks = weight_blocks(
        [after(array, scatters[1].moved) for array in grad_units],
        rows_in,
        [after(array, scatters[1].moved) for array in hidden],
        grads_in,
        planes,
    )

    far_first = scatters[1].first()
    scatters[0].first(*far_first)
    near_sum = scatters[0].total()
    far_sum = scatters[1].total()

    def from_far(total):
        return swap_halves(cross(total.astype(BF16), top)).astype(F32)

    out_far = [dot(after(h, far_sum), down_full, 0, 0).astype(BF16) for h in hidden[2:]]
    from_far_sum = from_far(far_sum)
    out_far = Scatter(*out_far, from_far_sum)
    out_far.first()
    unit_blocks = [after(part, far_sum) for part in unit_blocks]

    grad_normed_two = near_sum + from_far_sum
    grad_unit = grad_normed_two * gain_pair[1]
    gain_two_sum = jnp.sum(grad_normed_two * unit_two, axis=0)
    grad_middle = cotangent.astype(F32) + scale_two * (
        grad_unit - unit_two * jnp.mean(grad_unit * unit_two, axis=-1, keepdims=True)
    )
    branch_own = grad_middle.astype(BF16)

    branch = gather_end(branch_own, gather_begin(branch_own))
    grad_attended = jnp.concatenate(
        [dot(out_full, rows, 0, 1).astype(BF16) for rows in branch], axis=1
    )

    out_far = out_far.total(branch[0])
    out_near = [dot(after(h, grad_attended), down_full, 0, 0).astype(BF16) for h in hidden[:2]]
    out_near = Scatter(*out_near)

    grad_query, grad_pair = attention_backward(
        seq_at,
        starts,
        query,
        key,
        key_t,
        value,
        lse,
        grad_attended,
        cosine,
        sine,
        heads,
        share,
        size,
        documents,
    )
    unit_sums = dp_scatter(unit_blocks)
    inner = lane % share
    chunks = grad_pair.reshape(share, kept, length)
    pair_sum = lax.dynamic_index_in_dim(chunks, inner, 0, keepdims=False)
    for mask in range(1, share):
        chunk = lax.dynamic_index_in_dim(chunks, inner ^ mask, 0, keepdims=False)
        pair_sum = pair_sum + swap(chunk, mask)
    grad_mixed = jnp.concatenate([grad_query, pair_sum.astype(BF16)], axis=0)
    grad_mixed = after(grad_mixed, out_far)

    def own_columns(array):
        pair = lax.dynamic_slice_in_dim(array[:, columns:], inner * kept, kept, 1)
        return jnp.concatenate([array[:, :columns], pair], axis=1)

    grad_out_full = sum(dot(rows, part, 0, 0) for rows, part in zip(branch, halves(attended)))
    both_full = jnp.concatenate(
        [grad_out_full.astype(BF16), dot(normed, grad_mixed, 0, 1).astype(BF16)], axis=1
    )
    own_full = own_columns(qkv_full)
    grad_normed = Scatter(
        *[
            dot(part, own_full, 0, 1).astype(BF16)
            for part in (grad_mixed[:, :side], grad_mixed[:, side:])
        ]
    )
    first = grad_normed.first()
    out_near.first(*first)
    both = dp_scatter([both_full[k * block : (k + 1) * block] for k in range(planes)], *first)
    out_far = after(cross(out_far.astype(BF16), top), both[1])
    output = plain_output(middle, out_near.total(), out_far)
    both = both[0].astype(F32) + both[1].astype(F32)
    reduced_out, reduced_qkv = both[:, :columns], both[:, columns:]
    grad_normed = grad_normed.total()
    unit_sums = [after(part, both_full) for part in unit_sums]

    def whole_units(low, high):
        pair = [part[low:high].astype(F32) for part in unit_sums]
        return jnp.where(
            half == 0, jnp.concatenate(pair, axis=0), jnp.concatenate(pair[::-1], axis=0)
        )

    reduced_gate_up = jnp.stack([whole_units(0, few), whole_units(few, 2 * few)])
    reduced_down = whole_units(2 * few, 3 * few)
    unit_one = tokens.astype(F32)
    scale_own = lax.rsqrt(jnp.mean(unit_one * unit_one, axis=-1, keepdims=True) + rms_eps)
    unit_one = unit_one * scale_own
    grad_unit = grad_normed * gain_pair[0]
    input_grad = grad_middle + scale_own * (
        grad_unit - unit_one * jnp.mean(grad_unit * unit_one, axis=-1, keepdims=True)
    )
    input_grad = reorder_columns(input_grad)

    gain_one = jnp.sum(own_columns(own_qkv[:block]).astype(F32) * reduced_qkv, axis=1)
    gain_one = (gain_one / gain_pair[0, :block]).reshape(block // 128, 128)
    gain_two_sum = reorder_columns(jnp.broadcast_to(gain_two_sum, (8, width)))[0]
    squares = sum(
        jnp.sum(part * part) for part in (reduced_qkv, reduced_out, reduced_gate_up, reduced_down)
    )
    carried = jnp.concatenate(
        [
            gain_two_sum.reshape(width // 128, 128),
            jnp.broadcast_to(squares, (8, 128)),
            gain_one,
        ],
        axis=0,
    )
    carried = after(carried, output, input_grad)
    mask = 1
    while mask < lanes:
        carried = carried + swap(carried, mask)
        mask *= 2
    lines = width // 128
    seq_done = carried
    gain_one = carried[lines + 8 :]
    carried = jnp.concatenate(
        [carried[:lines], carried[lines : lines + 8] + jnp.sum(gain_one * gain_one)], axis=0
    )
    mask = 1
    while mask < planes:
        carried = carried + lax.ppermute(
            carried, "dp", [(at, at ^ mask) for at in range(planes)]
        )
        mask *= 2
    gain_two = carried[:lines]
    squares = carried[lines:] + jnp.sum(gain_two * gain_two)
    grad_norm = jnp.sqrt(squares[0, 0])
    factor = jnp.minimum(1.0, clip_limit / grad_norm)

    sent = lax.all_to_all(
        after(both.astype(BF16).reshape(lanes, owned, 2 * columns + kept), seq_done),
        "seq",
        split_axis=0,
        concat_axis=0,
        tiled=True,
    )
    out_grad = sent[:, :, :columns].transpose(1, 0, 2).reshape(owned, query_width).T.astype(F32)
    sent = sent[:, :, columns:]
    query_grad = sent[:, :, :columns].transpose(1, 0, 2).reshape(owned, query_width)
    pair_grad = (
        sent[:, :, columns:]
        .reshape(KEY_VALUE_HEADS, share, owned, kept)
        .transpose(2, 0, 1, 3)
        .reshape(owned, KEY_VALUE_HEADS, 2, HEAD_SIZE)
        .transpose(0, 2, 1, 3)
        .reshape(owned, 2 * pair_width)
    )
    qkv_grad = jnp.concatenate([query_grad, pair_grad], axis=1).astype(F32)
    gate_up_grad = reduced_gate_up.transpose(2, 0, 1)
    gains_grad = jnp.stack(
        [
            lax.dynamic_slice_in_dim(gain_one.reshape(block), lane * owned, owned, 0),
            lax.dynamic_slice_in_dim(
                gain_two.reshape(width), (plane * lanes + lane) * owned, owned, 0
            ),
        ]
    )

    reduced = (qkv_grad, out_grad, gate_up_grad, reduced_down, gains_grad)
    clipped = tuple(factor * gradient for gradient in reduced)
    masters = (query_key_value_weight, out_weight, gate_up_weight, down_weight, gains)
    firsts = (first_moment_query_key_value, first_out, first_gate_up, first_down, first_gains)
    seconds = (second_moment_query_key_value, second_out, second_gate_up, second_down, second_gains)
    averages = (average_query_key_value, average_out, average_gate_up, average_down, average_gains)
    results = [
        adam_update(
            masters[slot], clipped[slot], firsts[slot], seconds[slot], averages[slot], rates()[slot]
        )
        for slot in range(5)
    ]
    return (output, input_grad, grad_norm) + clipped + tuple(
        results[slot][part] for part in range(4) for slot in range(5)
    )


def solution(mesh):
    rows = P(("dp", "seq"), None)
    weights = (rows, P(None, ("dp", "seq")), P("dp", None, "seq"), P("seq", "dp"))
    weights = weights + (P(None, ("dp", "seq")),)
    return jax.shard_map(
        on_device,
        mesh=mesh,
        in_specs=(rows, rows, P("dp", None)) + weights * 4,
        out_specs=(rows, rows, P()) + weights * 5,
        check_vma=False,
    )
```

```python
import functools

import jax
import jax.numpy as jnp
from jax import lax
from jax.experimental import pallas as pl
from jax.experimental.pallas import tpu as pltpu
from jax.sharding import PartitionSpec as P

MODEL_WIDTH = 2048
FF = 5632
QUERY_HEAD_COUNT = 32
KEY_VALUE_HEADS = 4
HEAD_SIZE = 64
STEP = 10

rms_eps = 1e-05
rope_base = 10000.0
clip_limit = 1.0
beta_one = 0.9
beta_two = 0.95
adam_eps = 1e-08
weight_decay = 0.1
ema_decay = 0.8
masked_score = -1e30

HALF = HEAD_SIZE // 2
SCALE = HEAD_SIZE ** (-0.5)
F32 = jnp.float32
BF16 = jnp.bfloat16


def dot(left, right, left_dim, right_dim):
    return lax.dot_general(
        left, right, (((left_dim,), (right_dim,)), ((), ())), preferred_element_type=F32
    )


def swap(value, mask):
    count = lax.axis_size("seq")
    return lax.ppermute(value, "seq", [(at, at ^ mask) for at in range(count)])


def seq_order(count):
    return list(range(0, count, 2)) + list(range(1, count, 2))


def assemble_kernel(plan, *refs):
    for k, spans in enumerate(plan):
        at = 0
        for piece, low, high in spans:
            refs[len(refs) - len(plan) + k][at : at + high - low, :] = refs[piece][low:high, :]
            at += high - low


def assemble(pieces, plan=None):
    plan = plan or [[(k, 0, piece.shape[0]) for k, piece in enumerate(pieces)]]
    width, kind = pieces[0].shape[1], pieces[0].dtype
    shapes = [(sum(high - low for _, low, high in spans), width) for spans in plan]
    return pl.pallas_call(
        functools.partial(assemble_kernel, plan),
        out_shape=[jax.ShapeDtypeStruct(shape, kind) for shape in shapes],
        in_specs=[pl.BlockSpec(memory_space=pltpu.VMEM)] * len(pieces),
        out_specs=[pl.BlockSpec(memory_space=pltpu.VMEM)] * len(plan),
        cost_estimate=pl.CostEstimate(
            flops=0,
            bytes_accessed=4 * width * sum(shape[0] for shape in shapes),
            transcendentals=0,
        ),
        name="assemble",
    )(*pieces)


def gather_begin(rows):
    count = lax.axis_size("seq")
    if count != 8:
        return tuple(swap(rows, mask) for mask in range(2, count, 2))
    return swap(rows, 2), swap(rows, 4)


def gather_end(rows, first, *events):
    if lax.axis_size("seq") != 8:
        mine = assemble((rows,) + first)[0]
    else:
        half = rows.shape[0] // 2
        upper, lower = swap(first[0][:half], 4), swap(first[1][half:], 2)
        mine = assemble([rows, first[0], first[1], upper, lower])[0]
    return mine, swap(after(mine, *events) if events else mine, 1)


def seq_gather_two(one, two, *events):
    if lax.axis_size("seq") != 8:
        return tuple(gather_end(rows, gather_begin(rows)) for rows in (one, two))
    size = one.shape[0]
    rows = jnp.concatenate([one, two], axis=0)
    rows = after(rows, *events) if events else rows
    by_x, by_y = swap(rows, 2), swap(rows, 4)
    upper, lower = swap(by_x[:size], 4), swap(by_y[size:], 2)
    plan = [
        [(0, 0, size), (2, 0, size), (3, 0, size), (4, 0, size)],
        [(1, 0, size), (2, size, 2 * size), (3, size, 2 * size), (5, 0, size)],
    ]
    one, two = assemble([one, two, by_x, by_y, upper, lower], plan)
    return (one, swap(one, 1)), (two, swap(two, 1))


class Scatter:
    def __init__(self, mine, other, *events):
        self.mine, self.moved = mine, swap(after(other, *events) if events else other, 1)
        self.count = lax.axis_size("seq")
        self.size = 2 * mine.shape[0] // self.count

    def slot(self, mask, low=0, high=1):
        at, half = (mask // 2) * self.size, self.size // 2
        span = slice(at + low * half, at + high * half)
        return self.mine[span].astype(F32) + self.moved[span].astype(F32)

    def first(self, *events):
        if self.count != 8:
            return (self.moved,)
        slot = self.slot
        by_x = jnp.concatenate([slot(6), slot(2)], axis=0).astype(BF16)
        by_y = jnp.concatenate([slot(6, 1, 2), slot(4, 1, 2)], axis=0).astype(BF16)
        if events:
            by_x, by_y = after(by_x, *events), after(by_y, *events)
        self.by_x, self.by_y = swap(by_x, 2), swap(by_y, 4)
        return self.by_x, self.by_y

    def total(self, *events):
        slot, half = self.slot, self.size // 2
        if self.count != 8:
            total = slot(0, 0, 2)
            for mask in range(2, self.count, 2):
                total = total + swap(slot(mask, 0, 2).astype(BF16), mask).astype(F32)
            return total
        by_x = (slot(2, 1, 2) + self.by_y[:half].astype(F32)).astype(BF16)
        by_y = (slot(4) + self.by_x[:half].astype(F32)).astype(BF16)
        if events:
            by_x, by_y = after(by_x, *events), after(by_y, *events)
        by_x, by_y = swap(by_x, 2), swap(by_y, 4)
        upper = slot(0) + self.by_x[half:].astype(F32) + by_y.astype(F32)
        lower = slot(0, 1, 2) + self.by_y[half:].astype(F32) + by_x.astype(F32)
        return jnp.concatenate([upper, lower], axis=0)


def after(value, *events):
    return lax.optimization_barrier((value,) + events)[0]


def cross(value, mask):
    count = lax.axis_size("dp")
    return lax.ppermute(value, "dp", [(at, at ^ mask) for at in range(count)])


def dp_send(own, other):
    top = lax.axis_size("dp") // 2
    parts = {0: own, top: cross(other, top)}
    if top > 1:
        parts[1] = cross(own, 1)
    return parts


def dp_finish(parts):
    top = lax.axis_size("dp") // 2
    bit = 1
    while bit < top:
        for k in sorted(parts):
            if k ^ bit not in parts:
                parts[k ^ bit] = cross(parts[k], bit)
        bit *= 2
    return [parts[k] for k in range(2 * top)]


def dp_scatter(blocks, *events):
    top = lax.axis_size("dp") // 2
    kind = blocks[0].dtype
    blocks = {k: part for k, part in enumerate(blocks)}
    bit = top // 2
    while bit:
        for k in sorted(blocks, reverse=True):
            if k & bit:
                moved = cross(blocks[k], bit).astype(F32)
                blocks[k ^ bit] = (blocks[k ^ bit].astype(F32) + moved).astype(kind)
                del blocks[k]
        bit //= 2
    last = blocks[top].astype(kind)
    return blocks[0], cross(after(last, *events) if events else last, top)


def reorder_kernel(count, plane_ref, in_ref, out_ref):
    block = in_ref.shape[1] // count
    for k in range(count):
        source = pl.multiple_of(lax.bitwise_xor(plane_ref[0], k) * block, block)
        out_ref[:, k * block : (k + 1) * block] = in_ref[:, pl.ds(source, block)]


def reorder_columns(value):
    plane = lax.axis_index("dp").astype(jnp.int32).reshape(1)
    return pl.pallas_call(
        functools.partial(reorder_kernel, lax.axis_size("dp")),
        out_shape=jax.ShapeDtypeStruct(value.shape, value.dtype),
        in_specs=[pl.BlockSpec(memory_space=pltpu.SMEM), pl.BlockSpec(memory_space=pltpu.VMEM)],
        out_specs=pl.BlockSpec(memory_space=pltpu.VMEM),
        name="reorder",
    )(plane, value)


def output_kernel(count, plane_ref, middle_ref, near_ref, far_ref, out_ref):
    block = middle_ref.shape[1] // count
    for k in range(count):
        at = lax.bitwise_xor(plane_ref[0], k)
        span = pl.ds(pl.multiple_of(at * block, block), block)
        paired = lax.bitwise_xor(at, count // 2)
        far = far_ref[:, pl.ds(pl.multiple_of(paired * block, block), block)].astype(F32)
        total = middle_ref[:, span] + near_ref[:, span] + far
        out_ref[:, k * block : (k + 1) * block] = total.astype(BF16)


def plain_output(middle, near, far):
    plane = lax.axis_index("dp").astype(jnp.int32).reshape(1)
    return pl.pallas_call(
        functools.partial(output_kernel, lax.axis_size("dp")),
        out_shape=jax.ShapeDtypeStruct(middle.shape, BF16),
        in_specs=[pl.BlockSpec(memory_space=pltpu.SMEM)]
        + [pl.BlockSpec(memory_space=pltpu.VMEM)] * 3,
        out_specs=pl.BlockSpec(memory_space=pltpu.VMEM),
        name="plain_output",
    )(plane, middle, near, far)


def swap_halves(value):
    return jnp.roll(value, value.shape[1] // 2, axis=1)


def block_rows(length):
    return min(256, length)


def slot_place(lane, chunk, count, size):
    mask = lax.bitwise_xor(lane, chunk)
    odd = lax.bitwise_and(mask, 1)
    slot = lax.shift_right_logical(mask, 1) + odd * (count // 2)
    return pl.ds(pl.multiple_of(slot * size, size), size)


def slot_span(seq_ref, chunk, count, size):
    return slot_place(seq_ref[0], chunk, count, size)


def allowed_pairs(start_ref, documents, row_from, width, rows):
    key_at = lax.broadcasted_iota(jnp.int32, (width, rows), 0)
    query_at = row_from + lax.broadcasted_iota(jnp.int32, (width, rows), 1)
    allowed = key_at <= query_at
    if documents > 1:
        allowed = allowed & (key_at >= start_ref[:, row_from : row_from + rows])
    return allowed


def forward_kernel(
    heads,
    size,
    documents,
    seq_ref,
    start_ref,
    mixed_ref,
    cos_ref,
    sin_ref,
    out_ref,
    query_ref,
    key_ref,
    key_t_ref,
    value_ref,
    value_t_ref,
    lse_ref,
    gathered,
):
    length = mixed_ref.shape[1]
    width = heads * HEAD_SIZE
    for chunk in range(length // size):
        source = slot_span(seq_ref, chunk, length // size, size)
        place = slice(chunk * size, (chunk + 1) * size)
        cosine, sine = cos_ref[:, place], sin_ref[:, place]
        for head in range(heads + 1):
            base = head * HEAD_SIZE
            one = mixed_ref[base : base + HALF, source]
            two = mixed_ref[base + HALF : base + HEAD_SIZE, source]
            turned = jnp.concatenate(
                [one * cosine - two * sine, two * cosine + one * sine], axis=0
            ).astype(BF16)
            if head < heads:
                query_ref[base : base + HEAD_SIZE, place] = turned
            else:
                key_t_ref[:, place] = turned
        value_t_ref[:, place] = mixed_ref[width + HEAD_SIZE : width + 2 * HEAD_SIZE, source].astype(
            BF16
        )
    key_ref[...] = key_t_ref[...].astype(F32).T.astype(BF16)
    value_ref[...] = value_t_ref[...].astype(F32).T.astype(BF16)
    rows = block_rows(length)
    for block in range(length // rows):
        place = slice(block * rows, (block + 1) * rows)
        reach = (block + 1) * rows
        allowed = allowed_pairs(start_ref, documents, block * rows, reach, rows)
        for head in range(heads):
            span = slice(head * HEAD_SIZE, (head + 1) * HEAD_SIZE)
            query = query_ref[span, place] * jnp.asarray(SCALE, BF16)
            scores = jnp.where(allowed, dot(key_ref[:reach], query, 1, 0), masked_score)
            peak = jnp.max(scores, axis=0, keepdims=True)
            raised = jnp.exp(scores - peak)
            total = jnp.sum(raised, axis=0, keepdims=True)
            lse_ref[head : head + 1, place] = peak + jnp.log(total)
            weights = (raised * (1.0 / total)).astype(BF16)
            gathered[span, :] = dot(value_t_ref[:, :reach], weights, 1, 0)
        out = gathered[...].T.astype(BF16)
        for piece in range(rows // size):
            target = slot_span(
                seq_ref, block * (rows // size) + piece, length // size, size
            )
            out_ref[target, :] = out[piece * size : (piece + 1) * size]


def backward_kernel(
    heads,
    share,
    size,
    documents,
    seq_ref,
    start_ref,
    query_ref,
    key_ref,
    key_t_ref,
    value_ref,
    lse_ref,
    grad_ref,
    cos_ref,
    sin_ref,
    grad_query_ref,
    grad_pair_ref,
    grad_key,
    grad_value,
):
    length = query_ref.shape[1]
    rows = block_rows(length)
    pieces = rows // size
    grad_key[...] = jnp.zeros_like(grad_key)
    grad_value[...] = jnp.zeros_like(grad_value)
    for block in range(length // rows):
        place = slice(block * rows, (block + 1) * rows)
        reach = (block + 1) * rows
        allowed = allowed_pairs(start_ref, documents, block * rows, reach, rows)
        cosine, sine = cos_ref[:, place], sin_ref[:, place]
        spans = [
            slot_span(seq_ref, block * pieces + piece, length // size, size)
            for piece in range(pieces)
        ]
        for head in range(heads):
            base = head * HEAD_SIZE
            span = slice(base, base + HEAD_SIZE)
            query = query_ref[span, place] * jnp.asarray(SCALE, BF16)
            grad = jnp.concatenate([grad_ref[span, where] for where in spans], axis=1)
            scores = jnp.where(allowed, dot(key_ref[:reach], query, 1, 0), masked_score)
            weights = jnp.exp(scores - lse_ref[head : head + 1, place])
            slope = dot(value_ref[:reach], grad, 1, 0)
            delta = jnp.sum(weights * slope, axis=0, keepdims=True)
            inner = (weights * (slope - delta)).astype(BF16)
            pulled = (dot(key_t_ref[:, :reach], inner, 1, 0) * SCALE).astype(BF16).astype(F32)
            one, two = pulled[:HALF], pulled[HALF:]
            turned = jnp.concatenate(
                [one * cosine + two * sine, two * cosine - one * sine], axis=0
            ).astype(BF16)
            for piece, where in enumerate(spans):
                grad_query_ref[span, where] = turned[:, piece * size : (piece + 1) * size]
            grad_key[:reach] += dot(inner, query, 1, 1)
            grad_value[:reach] += dot(weights.astype(BF16), grad, 1, 1)
    key_t = grad_key[...].T
    value_t = grad_value[...].T
    one, two = key_t[:HALF], key_t[HALF:]
    cosine, sine = cos_ref[...], sin_ref[...]
    turned = jnp.concatenate([one * cosine + two * sine, two * cosine - one * sine], axis=0)
    both = jnp.concatenate([turned, value_t], axis=0)
    kept = 2 * HEAD_SIZE // share
    first_sharer = seq_ref[0] - lax.rem(seq_ref[0], share)
    for sharer in range(share):
        span = slice(sharer * kept, (sharer + 1) * kept)
        for chunk in range(length // size):
            target = slot_place(first_sharer + sharer, chunk, length // size, size)
            grad_pair_ref[span, target] = both[span, chunk * size : (chunk + 1) * size]


def weight_kernel(count, parts, *refs):
    left, right = refs[:parts], refs[parts : 2 * parts]
    left_two, right_two = refs[2 * parts : 3 * parts], refs[3 * parts : 4 * parts]
    outs = refs[4 * parts :]
    split = left[0].shape[0]
    one = dot(left[0][...], right[0][...], 1, 0)
    two = dot(left_two[0][...], right_two[0][...], 1, 0)
    for part in range(1, parts):
        one = one + dot(left[part][...], right[part][...], 1, 0)
        two = two + dot(left_two[part][...], right_two[part][...], 1, 0)
    for k in range(count):

        @pl.when(pl.program_id(0) == k)
        def _():
            outs[k][:split, :] = one.astype(BF16)
            outs[k][split:, :] = two.astype(BF16)


def weight_blocks(left, right, left_two, right_two, count):
    rows, depth = left[0].shape
    rows_two = left_two[0].shape[0]
    block = right[0].shape[1] // count
    parts = len(left)

    def specs(height):
        return [pl.BlockSpec((height, depth), lambda k: (0, 0))] * parts + [
            pl.BlockSpec((depth, block), lambda k: (0, k))
        ] * parts

    return pl.pallas_call(
        functools.partial(weight_kernel, count, parts),
        grid=(count,),
        out_shape=[jax.ShapeDtypeStruct((rows + rows_two, block), BF16)] * count,
        in_specs=specs(rows) + specs(rows_two),
        out_specs=[pl.BlockSpec((rows + rows_two, block), lambda k: (0, 0))] * count,
        compiler_params=pltpu.CompilerParams(vmem_limit_bytes=48 << 20),
        cost_estimate=pl.CostEstimate(
            flops=2 * (rows + rows_two) * depth * parts * block * count,
            bytes_accessed=4 * parts * depth * block * count,
            transcendentals=0,
        ),
        name="weight_blocks",
    )(*left, *right, *left_two, *right_two)


def attention_cost(heads, length, dots):
    return pl.CostEstimate(
        flops=dots * heads * length * length * 256,
        bytes_accessed=8 * length * heads * HEAD_SIZE,
        transcendentals=heads * length * length,
    )


def vmem_specs(count):
    return [pl.BlockSpec(memory_space=pltpu.VMEM)] * count


def attention_forward(seq_at, starts, mixed, cosine, sine, heads, size, documents):
    length = mixed.shape[1]
    width = heads * HEAD_SIZE
    shape = jax.ShapeDtypeStruct
    return pl.pallas_call(
        functools.partial(forward_kernel, heads, size, documents),
        out_shape=[
            shape((length, width), BF16),
            shape((width, length), BF16),
            shape((length, HEAD_SIZE), BF16),
            shape((HEAD_SIZE, length), BF16),
            shape((length, HEAD_SIZE), BF16),
            shape((HEAD_SIZE, length), BF16),
            shape((8, length), F32),
        ],
        in_specs=[pl.BlockSpec(memory_space=pltpu.SMEM)] + vmem_specs(4),
        out_specs=vmem_specs(7),
        scratch_shapes=[pltpu.VMEM((width, block_rows(length)), F32)],
        compiler_params=pltpu.CompilerParams(vmem_limit_bytes=40 << 20),
        cost_estimate=attention_cost(heads, length, 2),
        name="attention_forward",
    )(seq_at, starts, mixed, cosine, sine)


def attention_backward(
    seq_at, starts, query, key, key_t, value, lse, grad, cosine, sine, heads, share, size, documents
):
    width, length = query.shape
    shape = jax.ShapeDtypeStruct
    return pl.pallas_call(
        functools.partial(backward_kernel, heads, share, size, documents),
        out_shape=[shape((width, length), BF16), shape((2 * HEAD_SIZE, length), F32)],
        in_specs=[pl.BlockSpec(memory_space=pltpu.SMEM)] + vmem_specs(9),
        out_specs=vmem_specs(2),
        scratch_shapes=[pltpu.VMEM((length, HEAD_SIZE), F32)] * 2,
        compiler_params=pltpu.CompilerParams(vmem_limit_bytes=40 << 20),
        cost_estimate=attention_cost(heads, length, 5),
        name="attention_backward",
    )(seq_at, starts, query, key, key_t, value, lse, grad, cosine, sine)


def rates():
    return (
        0.5 * (2.0 / MODEL_WIDTH) ** 0.5,
        0.5 * (16.0 / (QUERY_HEAD_COUNT * HEAD_SIZE)) ** 0.5,
        0.5 * (1.0 / MODEL_WIDTH) ** 0.5,
        0.5 * (1.0 / FF) ** 0.5,
        0.3,
    )


def adam_update(weight, gradient, moment_one, moment_two, average, rate):
    first_new = beta_one * moment_one + (1.0 - beta_one) * gradient
    second_new = beta_two * moment_two + (1.0 - beta_two) * gradient * gradient
    corrected = (
        first_new
        / (1.0 - beta_one**STEP)
        / (jnp.sqrt(second_new / (1.0 - beta_two**STEP)) + adam_eps)
    )
    weight_new = weight - rate * (corrected + weight_decay * weight)
    average_new = ema_decay * average + (1.0 - ema_decay) * weight_new
    return (weight_new, first_new, second_new, average_new)


def on_device(
    tokens,
    cotangent,
    lengths,
    query_key_value_weight,
    out_weight,
    gate_up_weight,
    down_weight,
    gains,
    first_moment_query_key_value,
    first_out,
    first_gate_up,
    first_down,
    first_gains,
    second_moment_query_key_value,
    second_out,
    second_gate_up,
    second_down,
    second_gains,
    average_query_key_value,
    average_out,
    average_gate_up,
    average_down,
    average_gains,
):
    planes, lanes = lax.axis_size("dp"), lax.axis_size("seq")
    plane, lane = lax.axis_index("dp"), lax.axis_index("seq")
    size, width = tokens.shape
    length = size * lanes
    documents = lengths.shape[1]
    heads = QUERY_HEAD_COUNT // lanes
    columns = heads * HEAD_SIZE
    share = lanes // KEY_VALUE_HEADS
    kept = 2 * HEAD_SIZE // share
    every = columns + 2 * HEAD_SIZE
    owned = query_key_value_weight.shape[0]
    block = owned * lanes
    query_width = QUERY_HEAD_COUNT * HEAD_SIZE
    pair_width = KEY_VALUE_HEADS * HEAD_SIZE
    units = gate_up_weight.shape[2]
    seq_at = lane.astype(jnp.int32).reshape(1)

    qkv_b = query_key_value_weight.astype(BF16)
    query_part = qkv_b[:, :query_width].reshape(owned, lanes, columns)

    def per_device(part):
        part = part.reshape(owned, KEY_VALUE_HEADS, HEAD_SIZE)
        return jnp.repeat(part, share, axis=1)

    key_part = per_device(qkv_b[:, query_width : query_width + pair_width])
    value_part = per_device(qkv_b[:, query_width + pair_width :])
    message = jnp.concatenate([query_part, key_part, value_part], axis=2).transpose(1, 0, 2)
    gain_row = jnp.pad(gains.astype(BF16).reshape(1, 2 * owned), ((0, 7), (0, every - 2 * owned)))
    message = jnp.concatenate(
        [message, jnp.broadcast_to(gain_row[None], (lanes, 8, every))], axis=1
    )
    top = planes // 2
    half = plane // top
    tokens = reorder_columns(after(tokens, message))
    cotangent = reorder_columns(after(cotangent, message))
    grad_far = cross(swap_halves(cotangent), top)

    message = lax.all_to_all(message, "seq", split_axis=0, concat_axis=0, tiled=True)
    own_qkv = after(message[:, :owned].reshape(block, every), grad_far)
    own_qkv = jnp.concatenate([own_qkv, message[:, owned]], axis=0)
    qkv_parts = dp_send(own_qkv, own_qkv)
    qkv_events = list(qkv_parts.values())
    qkv_parts = dp_finish(qkv_parts)
    qkv_full = jnp.concatenate([part[:block] for part in qkv_parts], axis=0)
    gain_pair = jnp.concatenate(
        [
            part[block:, : 2 * owned].reshape(lanes, 2, owned).transpose(1, 0, 2).reshape(2, block)
            for part in qkv_parts
        ],
        axis=1,
    ).astype(F32)

    in_all = gather_end(tokens, gather_begin(tokens))
    grad_near, grad_far = seq_gather_two(cotangent, grad_far, own_qkv)

    out_b = out_weight.T.astype(BF16).reshape(owned, lanes, columns).transpose(1, 0, 2)
    out_b = lax.all_to_all(out_b, "seq", split_axis=0, concat_axis=0, tiled=True)
    out_b = after(out_b.reshape(block, columns), *qkv_events)
    out_parts = dp_send(out_b, out_b)
    out_events = list(out_parts.values())
    out_full = jnp.concatenate(dp_finish(out_parts), axis=0)

    few = units // 2

    def half_of(array, which):
        return lax.dynamic_slice_in_dim(array, which * few, few, array.ndim - 2)

    gate_up_b = gate_up_weight.transpose(1, 2, 0).astype(BF16)
    gate_up_near = half_of(gate_up_b, half).reshape(2 * few, block)
    gate_up_far = half_of(gate_up_b, 1 - half).reshape(2 * few, block)
    gate_up_parts = dp_send(after(gate_up_near, *qkv_events), after(gate_up_far, *qkv_events))
    gate_up_events = list(gate_up_parts.values())
    gate_up_parts = dp_finish(gate_up_parts)
    gate_up_last = gate_up_parts[-1]
    gate_up_full = jnp.concatenate(gate_up_parts, axis=1)
    down_b = down_weight.astype(BF16)
    down_parts = dp_send(
        after(half_of(down_b, half), *gate_up_events),
        after(half_of(down_b, 1 - half), *gate_up_events),
    )
    down_events = list(down_parts.values())
    down_parts = dp_finish(down_parts)
    down_last = down_parts[-1]
    down_full = jnp.concatenate(down_parts, axis=1)

    ends = jnp.cumsum(lengths[0])
    places = jnp.arange(length, dtype=jnp.int32)
    begins = (ends - lengths[0])[None, :]
    within = (places[:, None] >= begins) & (places[:, None] < ends[None, :])
    starts = jnp.sum(jnp.where(within, begins, 0), axis=1).astype(jnp.int32)
    frequency = rope_base ** (-2.0 * jnp.arange(HALF, dtype=F32) / HEAD_SIZE)
    phases = frequency[:, None] * (places - starts).astype(F32)[None, :]
    cosine, sine = jnp.cos(phases), jnp.sin(phases)
    starts = starts[None, :]

    gain_pair = after(gain_pair, grad_near[0], grad_far[0])

    def norm_one(rows):
        rows = rows.astype(F32)
        scale = lax.rsqrt(jnp.mean(rows * rows, axis=-1, keepdims=True) + rms_eps)
        return (rows * scale * gain_pair[0]).astype(BF16)

    normed = jnp.concatenate([norm_one(rows) for rows in in_all], axis=0)
    mixed = after(dot(qkv_full, normed, 0, 1), grad_near[1], grad_far[1])
    attended, query, key, key_t, value, _, lse = attention_forward(
        seq_at, starts, mixed, cosine, sine, heads, size, documents
    )
    side = length // 2

    def halves(array):
        return array[:side], array[side:]

    part = [dot(rows, out_full, 1, 1).astype(BF16) for rows in halves(attended)]
    scatter = Scatter(*part, *gate_up_events)
    scatter.first()
    middle = tokens.astype(F32) + scatter.total(*down_events)

    scale_two = lax.rsqrt(jnp.mean(middle * middle, axis=-1, keepdims=True) + rms_eps)
    unit_two = middle * scale_two
    normed_two = (unit_two * gain_pair[1]).astype(BF16)
    normed_far = cross(swap_halves(normed_two), top)
    near_first = gather_begin(after(normed_two, gate_up_last))
    near_first = lax.optimization_barrier(near_first + (down_last, normed_far))
    normed_far = near_first[-1]
    far_first = gather_begin(normed_far)
    normed_near = gather_end(normed_two, near_first[:-2], *far_first)
    normed_far = gather_end(normed_far, far_first)

    def feed_forward(rows, grads):
        gate_up = dot(gate_up_full, rows, 1, 1)
        gate, up = gate_up[:few], gate_up[few:]
        sigmoid = jax.nn.sigmoid(gate)
        hidden = (gate * sigmoid * up).astype(BF16)
        grad_hidden = dot(down_full, grads, 1, 1)
        grad_gate = grad_hidden * up * sigmoid * (1.0 + gate * (1.0 - sigmoid))
        grad_up = grad_hidden * gate * sigmoid
        grad_gate_up = jnp.concatenate([grad_gate.astype(BF16), grad_up.astype(BF16)], axis=0)
        return hidden, grad_gate_up, dot(grad_gate_up, gate_up_full, 0, 0).astype(BF16)

    rows_in = normed_near + normed_far
    grads_in = grad_near + grad_far
    done = [feed_forward(rows, grads) for rows, grads in zip(rows_in, grads_in)]
    hidden, grad_units, parts = zip(*done)
    scatters = [Scatter(parts[0], parts[1]), Scatter(parts[2], parts[3])]

    unit_blocks = weight_blocks(
        [after(array, scatters[1].moved) for array in grad_units],
        rows_in,
        [after(array, scatters[1].moved) for array in hidden],
        grads_in,
        planes,
    )

    far_first = scatters[1].first()
    scatters[0].first(*far_first)
    near_sum = scatters[0].total()
    far_sum = scatters[1].total()

    def from_far(total):
        return swap_halves(cross(total.astype(BF16), top)).astype(F32)

    out_far = [dot(after(h, far_sum), down_full, 0, 0).astype(BF16) for h in hidden[2:]]
    from_far_sum = from_far(far_sum)
    out_far = Scatter(*out_far, from_far_sum)
    out_far.first()
    unit_blocks = [after(part, far_sum) for part in unit_blocks]

    grad_normed_two = near_sum + from_far_sum
    grad_unit = grad_normed_two * gain_pair[1]
    gain_two_sum = jnp.sum(grad_normed_two * unit_two, axis=0)
    grad_middle = cotangent.astype(F32) + scale_two * (
        grad_unit - unit_two * jnp.mean(grad_unit * unit_two, axis=-1, keepdims=True)
    )
    branch_own = grad_middle.astype(BF16)

    branch = gather_end(branch_own, gather_begin(branch_own))
    grad_attended = jnp.concatenate(
        [dot(out_full, rows, 0, 1).astype(BF16) for rows in branch], axis=1
    )

    out_far = out_far.total(branch[0])
    out_near = [dot(after(h, grad_attended), down_full, 0, 0).astype(BF16) for h in hidden[:2]]
    out_near = Scatter(*out_near)

    grad_query, grad_pair = attention_backward(
        seq_at,
        starts,
        query,
        key,
        key_t,
        value,
        lse,
        grad_attended,
        cosine,
        sine,
        heads,
        share,
        size,
        documents,
    )
    unit_sums = dp_scatter(unit_blocks)
    inner = lane % share
    chunks = grad_pair.reshape(share, kept, length)
    pair_sum = lax.dynamic_index_in_dim(chunks, inner, 0, keepdims=False)
    for mask in range(1, share):
        chunk = lax.dynamic_index_in_dim(chunks, inner ^ mask, 0, keepdims=False)
        pair_sum = pair_sum + swap(chunk, mask)
    grad_mixed = jnp.concatenate([grad_query, pair_sum.astype(BF16)], axis=0)
    grad_mixed = after(grad_mixed, out_far)

    def own_columns(array):
        pair = lax.dynamic_slice_in_dim(array[:, columns:], inner * kept, kept, 1)
        return jnp.concatenate([array[:, :columns], pair], axis=1)

    grad_out_full = sum(dot(rows, part, 0, 0) for rows, part in zip(branch, halves(attended)))
    both_full = jnp.concatenate(
        [grad_out_full.astype(BF16), dot(normed, grad_mixed, 0, 1).astype(BF16)], axis=1
    )
    own_full = own_columns(qkv_full)
    grad_normed = Scatter(
        *[
            dot(part, own_full, 0, 1).astype(BF16)
            for part in (grad_mixed[:, :side], grad_mixed[:, side:])
        ]
    )
    first = grad_normed.first()
    out_near.first(*first)
    both = dp_scatter([both_full[k * block : (k + 1) * block] for k in range(planes)], *first)
    out_far = after(cross(out_far.astype(BF16), top), both[1])
    output = plain_output(middle, out_near.total(), out_far)
    both = both[0].astype(F32) + both[1].astype(F32)
    reduced_out, reduced_qkv = both[:, :columns], both[:, columns:]
    grad_normed = grad_normed.total()
    unit_sums = [after(part, both_full) for part in unit_sums]

    def whole_units(low, high):
        pair = [part[low:high].astype(F32) for part in unit_sums]
        return jnp.where(
            half == 0, jnp.concatenate(pair, axis=0), jnp.concatenate(pair[::-1], axis=0)
        )

    reduced_gate_up = jnp.stack([whole_units(0, few), whole_units(few, 2 * few)])
    reduced_down = whole_units(2 * few, 3 * few)
    unit_one = tokens.astype(F32)
    scale_own = lax.rsqrt(jnp.mean(unit_one * unit_one, axis=-1, keepdims=True) + rms_eps)
    unit_one = unit_one * scale_own
    grad_unit = grad_normed * gain_pair[0]
    input_grad = grad_middle + scale_own * (
        grad_unit - unit_one * jnp.mean(grad_unit * unit_one, axis=-1, keepdims=True)
    )
    input_grad = reorder_columns(input_grad)

    gain_one = jnp.sum(own_columns(own_qkv[:block]).astype(F32) * reduced_qkv, axis=1)
    gain_one = (gain_one / gain_pair[0, :block]).reshape(block // 128, 128)
    gain_two_sum = reorder_columns(jnp.broadcast_to(gain_two_sum, (8, width)))[0]
    squares = sum(
        jnp.sum(part * part) for part in (reduced_qkv, reduced_out, reduced_gate_up, reduced_down)
    )
    carried = jnp.concatenate(
        [
            gain_two_sum.reshape(width // 128, 128),
            jnp.broadcast_to(squares, (8, 128)),
            gain_one,
        ],
        axis=0,
    )
    carried = after(carried, output, input_grad)
    mask = 1
    while mask < lanes:
        carried = carried + swap(carried, mask)
        mask *= 2
    lines = width // 128
    seq_done = carried
    gain_one = carried[lines + 8 :]
    carried = jnp.concatenate(
        [carried[:lines], carried[lines : lines + 8] + jnp.sum(gain_one * gain_one)], axis=0
    )
    mask = 1
    while mask < planes:
        carried = carried + lax.ppermute(
            carried, "dp", [(at, at ^ mask) for at in range(planes)]
        )
        mask *= 2
    gain_two = carried[:lines]
    squares = carried[lines:] + jnp.sum(gain_two * gain_two)
    grad_norm = jnp.sqrt(squares[0, 0])
    factor = jnp.minimum(1.0, clip_limit / grad_norm)

    sent = lax.all_to_all(
        after(both.astype(BF16).reshape(lanes, owned, 2 * columns + kept), seq_done),
        "seq",
        split_axis=0,
        concat_axis=0,
        tiled=True,
    )
    out_grad = sent[:, :, :columns].transpose(1, 0, 2).reshape(owned, query_width).T.astype(F32)
    sent = sent[:, :, columns:]
    query_grad = sent[:, :, :columns].transpose(1, 0, 2).reshape(owned, query_width)
    pair_grad = (
        sent[:, :, columns:]
        .reshape(KEY_VALUE_HEADS, share, owned, kept)
        .transpose(2, 0, 1, 3)
        .reshape(owned, KEY_VALUE_HEADS, 2, HEAD_SIZE)
        .transpose(0, 2, 1, 3)
        .reshape(owned, 2 * pair_width)
    )
    qkv_grad = jnp.concatenate([query_grad, pair_grad], axis=1).astype(F32)
    gate_up_grad = reduced_gate_up.transpose(2, 0, 1)
    gains_grad = jnp.stack(
        [
            lax.dynamic_slice_in_dim(gain_one.reshape(block), lane * owned, owned, 0),
            lax.dynamic_slice_in_dim(
                gain_two.reshape(width), (plane * lanes + lane) * owned, owned, 0
            ),
        ]
    )

    reduced = (qkv_grad, out_grad, gate_up_grad, reduced_down, gains_grad)
    clipped = tuple(factor * gradient for gradient in reduced)
    masters = (query_key_value_weight, out_weight, gate_up_weight, down_weight, gains)
    firsts = (first_moment_query_key_value, first_out, first_gate_up, first_down, first_gains)
    seconds = (second_moment_query_key_value, second_out, second_gate_up, second_down, second_gains)
    averages = (average_query_key_value, average_out, average_gate_up, average_down, average_gains)
    results = [
        adam_update(
            masters[slot], clipped[slot], firsts[slot], seconds[slot], averages[slot], rates()[slot]
        )
        for slot in range(5)
    ]
    return (output, input_grad, grad_norm) + clipped + tuple(
        results[slot][part] for part in range(4) for slot in range(5)
    )


def solution(mesh):
    rows = P(("dp", "seq"), None)
    weights = (rows, P(None, ("dp", "seq")), P("dp", None, "seq"), P("seq", "dp"))
    weights = weights + (P(None, ("dp", "seq")),)
    return jax.shard_map(
        on_device,
        mesh=mesh,
        in_specs=(rows, rows, P("dp", None)) + weights * 4,
        out_specs=(rows, rows, P()) + weights * 5,
        check_vma=False,
    )
```
